32 devices in a mesh: dp: 8 (over z, y), rep: 4 (over x, core).
Axes of the slice: x: 2, y: 2, z: 4, core: 2. Of those that a mesh axis runs over, the one named last changes fastest.
Arguments:
- tokens: bfloat16 [1024, 2048], P('dp'), may hold values from -6 to 6
- cotangent: bfloat16 [1024, 2048], P('dp'), may hold values from -6 to 6
- probe_seed: int32 [1024], P('dp'), may hold values from 0 to 1073741823
- w_in: bfloat16 [2048, 8192], P('dp', 'rep'), may hold values from -0.125 to 0.125
- bias: float32 [8192], P('rep'), may hold values from -1.5 to 1.5
- w_out: bfloat16 [8192, 2048], P(('rep', 'dp')), may hold values from -0.0625 to 0.0625
- left_in: bfloat16 [2048], replicated, may hold values from -6 to 6
- left_out: bfloat16 [8192], P('rep'), may hold values from -6 to 6
Outputs:
- output: bfloat16 [1024, 2048], P('dp')
- logdet: float32 [1024], P('dp')
- grad_tokens: float32 [1024, 2048], P('dp')
- grad_in: float32 [2048, 8192], P('dp', 'rep')
- grad_out: float32 [8192, 2048], P(('rep', 'dp'))
The draws below stay inside these ranges and needn't reach their ends.
All inputs are finite; a program needn't handle non-finite values.
Results may differ from the reference program's by a relative error of at most 0.012.
Values may be sent and summed in bfloat16 or wider, within the bound.
No kernel may reach another device: no remote copies, remote signals or barrier semaphores. Data moves between devices by JAX's collectives and lax.ppermute only.
A program may use at most 128 MiB of HBM per device.

```python
import jax
import jax.numpy as jnp
from jax import lax

D = 2048
H = 8192
TOKENS = 1024


def with_ends(array, rng, smallest, high):
    index_at = [jax.random.randint(jax.random.fold_in(rng, axis), (), 0, length) for axis, length in enumerate(array.shape)]
    main_axis = array.shape.index(max(array.shape))
    neighbour = index_at[:main_axis] + [(index_at[main_axis] + 1) % array.shape[main_axis]] + index_at[main_axis + 1:]
    return array.at[tuple(index_at)].set(smallest).at[tuple(neighbour)].set(high)


def strengthened(result, rng, source, target, shards_of, factor):
    owner, partner = [(jnp.arange(result.shape[axis_at]) // (result.shape[axis_at] // shards_of)).reshape([-1 if axis == axis_at else 1 for axis in range(result.ndim)]) for axis_at in (source, target)]
    chosen = jax.random.permutation(rng, shards_of)[partner]
    strong = (owner == chosen) | (owner == (partner + shards_of // 2) % shards_of)
    return jnp.where(strong, factor * result, result)


def level_of(own_key, shape, cuts, least, largest):
    factor_of, own = 1.0, jax.random.fold_in(own_key, 6)
    for axis_at, parts in cuts:
        heights = jnp.exp(jax.random.uniform(jax.random.fold_in(own, axis_at), (parts,), jnp.float32, least / len(cuts), largest / len(cuts)))
        factor_of = factor_of * jnp.repeat(heights, shape[axis_at] // parts).reshape([-1 if axis == axis_at else 1 for axis in range(len(shape))])
    return factor_of


def bell_draw(stream_key, extent, spread, bound, cuts=(), held_as=jnp.bfloat16):
    gain = level_of(stream_key, extent, cuts, -0.22, 0.18) if cuts else 1.0
    array = jax.random.normal(stream_key, extent, jnp.float32) * spread * gain
    return jnp.minimum(jnp.maximum(array, -bound), bound).astype(held_as)


def bell_draw_with(own_key, shape, scale, reach, cuts, heavy, held_as=jnp.bfloat16):
    values = scale * jax.random.normal(own_key, shape, jnp.float32)
    if cuts:
        values = values * level_of(own_key, shape, cuts, -0.22, 0.18)
    return jnp.clip(strengthened(values, jax.random.fold_in(own_key, 3), *heavy), -reach, reach).astype(held_as)


def setup_inputs(seed: int = 0) -> dict:
    splits = jax.random.split(jax.random.key(seed), 9)
    tokens = bell_draw_with(splits[0], (TOKENS, D), 1.0, 6.0, ((0, 8),), (0, 1, 8, 2.0))
    cotangent = bell_draw(splits[1], (TOKENS, D), 1.0, 6.0, ((0, 8),))
    probe_seed = with_ends(jax.random.randint(splits[2], (TOKENS,), 0, 1073741824), jax.random.fold_in(splits[2], 1), 0, 1073741823).astype(jnp.int32)
    w_in = bell_draw(splits[3], (D, H), D ** -0.5, 0.125, ((0, 8), (1, 4)))
    bias = jnp.clip(jax.random.uniform(splits[4], (H,), jnp.float32, -1.5, 1.5) * level_of(splits[4], (H,), ((0, 4),), -0.4, 0.0), -1.5, 1.5)
    w_out = bell_draw(splits[5], (H, D), H ** -0.5, 0.0625, ((0, 32),))
    left_in = bell_draw(splits[6], (D,), 1.0, 6.0)
    left_out = bell_draw(splits[7], (H,), 1.0, 6.0, ((0, 4),))
    return {"tokens": tokens, "cotangent": cotangent, "probe_seed": probe_seed, "w_in": w_in, "bias": bias, "w_out": w_out, "left_in": left_in, "left_out": left_out}


def probe_signs(seeds, width):
    columns = jnp.arange(width, dtype=jnp.int32)
    mixed = seeds[:, None] * 747796405 + columns[None, :] * 1640531527
    mixed = mixed ^ lax.shift_right_logical(mixed, jnp.full_like(mixed, 16))
    mixed = mixed * 668265261
    mixed = mixed ^ lax.shift_right_logical(mixed, jnp.full_like(mixed, 15))
    lowbit = jnp.bitwise_and(lax.shift_right_logical(mixed, jnp.full_like(mixed, 7)), 1)
    return (1 - 2 * lowbit).astype(jnp.float32).astype(jnp.bfloat16)

def contract_rows(left, right):
    return lax.dot_general(left, right, (((0,), (0,)), ((), ())), preferred_element_type=jnp.float32)

def contract_cols(left, right):
    return lax.dot_general(left, right, (((1,), (1,)), ((), ())), preferred_element_type=jnp.float32)

def reference(tokens, cotangent, probe_seed, w_in, bias, w_out, left_in, left_out):
    coef = 0.9
    p_vec = jnp.dot(left_in, w_in, preferred_element_type=jnp.float32)
    q_vec = jnp.dot(left_out, w_out, preferred_element_type=jnp.float32)
    p_norm = jnp.sum(p_vec * p_vec)
    q_norm = jnp.sum(q_vec * q_vec)
    left_one = left_in.astype(jnp.float32)
    left_two = left_out.astype(jnp.float32)
    scale_in = coef * jnp.sqrt(jnp.sum(left_one * left_one) / p_norm)
    scale_out = coef * jnp.sqrt(jnp.sum(left_two * left_two) / q_norm)
    probe = probe_signs(probe_seed, D)
    z_pre = scale_in * jnp.dot(tokens, w_in, preferred_element_type=jnp.float32) + bias
    e_one = scale_in * jnp.dot(probe, w_in, preferred_element_type=jnp.float32)
    tanh_z = jnp.tanh(z_pre)
    deriv = 1.0 - tanh_z * tanh_z
    second = -2.0 * tanh_z * deriv
    act = tanh_z.astype(jnp.bfloat16)
    r_one = (e_one * deriv).astype(jnp.bfloat16)
    output = (tokens.astype(jnp.float32) + scale_out * jnp.dot(act, w_out, preferred_element_type=jnp.float32)).astype(jnp.bfloat16)
    j_one = (scale_out * jnp.dot(r_one, w_out, preferred_element_type=jnp.float32)).astype(jnp.bfloat16)
    e_two = scale_in * jnp.dot(j_one, w_in, preferred_element_type=jnp.float32)
    r_two = (e_two * deriv).astype(jnp.bfloat16)
    j_two = (scale_out * jnp.dot(r_two, w_out, preferred_element_type=jnp.float32)).astype(jnp.bfloat16)
    e_three = scale_in * jnp.dot(j_two, w_in, preferred_element_type=jnp.float32)
    bvec = scale_out * contract_cols(probe, w_out)
    cback = scale_out * contract_cols(cotangent, w_out)
    hd_vec = deriv * bvec
    term_one = lax.optimization_barrier(jnp.sum(e_one * hd_vec, axis=1))
    term_two = lax.optimization_barrier(jnp.sum(e_two * hd_vec, axis=1))
    term_three = lax.optimization_barrier(jnp.sum(e_three * hd_vec, axis=1))
    logdet = term_one - term_two / 2.0 + term_three / 3.0
    a_vec = e_one - e_two + e_three
    dz_vec = cback * deriv - a_vec * bvec * second
    dz_round = dz_vec.astype(jnp.bfloat16)
    grad_tokens = cotangent.astype(jnp.float32) + scale_in * contract_cols(dz_round, w_in)
    w_vec = (probe.astype(jnp.float32) - j_one.astype(jnp.float32) + j_two.astype(jnp.float32)).astype(jnp.bfloat16)
    h_round = hd_vec.astype(jnp.bfloat16)
    g_round = (a_vec * deriv).astype(jnp.bfloat16)
    left_grad = jnp.concatenate([tokens, w_vec], 0)
    right_grad = jnp.concatenate([dz_round, -h_round], 0)
    left_two_grad = jnp.concatenate([act, g_round], 0)
    right_two_grad = jnp.concatenate([cotangent, -probe], 0)
    grad_one = contract_rows(left_grad, right_grad)
    grad_two = contract_rows(left_two_grad, right_two_grad)
    inner_one = jnp.sum(grad_one * w_in.astype(jnp.float32))
    inner_two = jnp.sum(grad_two * w_out.astype(jnp.float32))
    grad_in = scale_in * (grad_one - inner_one * left_one[:, None] * p_vec[None, :] / p_norm)
    grad_out = scale_out * (grad_two - inner_two * left_two[:, None] * q_vec[None, :] / q_norm)
    return (output, logdet, grad_tokens, grad_in, grad_out)
```

```python
import jax
import jax.numpy as jnp
from jax import lax
from jax.sharding import Mesh
from jax.sharding import PartitionSpec as P

F32 = jnp.float32
BF16 = jnp.bfloat16
EVERY = ("z", "y", "x", "c")
SWAP = [(0, 1), (1, 0)]


def probe_signs(seeds, width):
    columns = jnp.arange(width, dtype=jnp.int32)
    mixed = seeds[:, None] * 747796405 + columns[None, :] * 1640531527
    mixed = mixed ^ lax.shift_right_logical(mixed, jnp.full_like(mixed, 16))
    mixed = mixed * 668265261
    mixed = mixed ^ lax.shift_right_logical(mixed, jnp.full_like(mixed, 15))
    lowbit = jnp.bitwise_and(lax.shift_right_logical(mixed, jnp.full_like(mixed, 7)), 1)
    return (1 - 2 * lowbit).astype(F32).astype(BF16)


def times(left, right):
    return jnp.dot(left, right, preferred_element_type=F32)


def contract_rows(left, right):
    return lax.dot_general(left, right, (((0,), (0,)), ((), ())), preferred_element_type=F32)


def contract_cols(left, right):
    return lax.dot_general(left, right, (((1,), (1,)), ((), ())), preferred_element_type=F32)


def in_order(own, other, index):
    first = jnp.where(index == 0, own, other)
    second = jnp.where(index == 0, other, own)
    return jnp.concatenate([first, second], 0)


def scatter_sum(part, planes, core):
    half = part.shape[0] // 2
    keep = lax.dynamic_slice_in_dim(part, core * half, half, 0)
    give = lax.dynamic_slice_in_dim(part, (1 - core) * half, half, 0).astype(BF16)
    pair = (keep + lax.ppermute(give, "c", SWAP).astype(F32)).astype(BF16)
    got = lax.all_to_all(pair, "z", 0, 0, tiled=True)
    return jnp.sum(got.reshape(planes, half // planes, -1).astype(F32), 0)


def gather_rows(quarter, core):
    half = lax.all_gather(quarter, "z", axis=0, tiled=True)
    return in_order(half, lax.ppermute(half, "c", SWAP), core)


def on_device(tokens, cotangent, probe_seed, w_in, bias, w_out, left_in, left_out):
    coef = 0.9
    planes = lax.axis_size("z")
    at_z, at_y, at_x, core = (lax.axis_index(name) for name in EVERY)
    count, width = tokens.shape
    rows_in, hid_rep = w_in.shape
    rows_out = w_out.shape[0]
    piece = hid_rep // planes
    quarter = count // 4
    at_dp = at_z * 2 + at_y
    at_rep = at_x * 2 + core

    full_out = lax.all_gather(w_out, ("x", "y"), axis=0, tiled=True)
    in_z = lax.all_to_all(w_in, "z", 1, 0, tiled=True)
    in_xy = lax.all_gather(in_z, ("x", "y"), axis=0)
    full_in = (
        in_xy.reshape(2, 2, planes, rows_in, piece)
        .transpose(2, 1, 3, 0, 4)
        .reshape(width, 2 * piece)
    )

    def own_quarter(array):
        return lax.dynamic_slice_in_dim(array, at_rep * quarter, quarter, 0)

    tok_own = own_quarter(tokens)
    pair = jnp.stack([tok_own, own_quarter(cotangent)])
    pair = lax.all_gather(pair, "z", axis=1)
    tok = in_order(pair[0], lax.ppermute(pair[0], "c", SWAP), core).reshape(-1, width)
    cot = in_order(pair[1], lax.ppermute(pair[1], "c", SWAP), core).reshape(-1, width)
    seeds = lax.all_gather(own_quarter(probe_seed), ("c", "z"), axis=0, tiled=True)
    probe = probe_signs(seeds, width)
    n = tok.shape[0]
    bias_all = lax.all_gather(
        lax.dynamic_slice_in_dim(bias, at_z * piece, piece, 0), "x", axis=0, tiled=True
    )

    left_one = left_in.astype(F32)
    slice_one = lax.dynamic_slice_in_dim(left_in, at_dp * rows_in, rows_in, 0)
    slice_two = lax.dynamic_slice_in_dim(left_out, at_dp * rows_out, rows_out, 0)
    p_part = times(slice_one, w_in)
    q_part = times(slice_two, w_out)
    slice_one = slice_one.astype(F32)
    slice_two = slice_two.astype(F32)
    reps = lax.axis_size("x") * 2
    p_slots = jnp.where(jnp.arange(reps)[:, None] == at_rep, p_part[None, :], 0.0)
    sums = lax.psum(
        jnp.concatenate([p_slots.reshape(-1), q_part, jnp.sum(slice_two * slice_two)[None]]), EVERY
    )
    p_all = sums[: reps * hid_rep].reshape(reps, hid_rep)
    q_vec = sums[reps * hid_rep : reps * hid_rep + width]
    p_norm = jnp.sum(p_all * p_all)
    q_norm = jnp.sum(q_vec * q_vec)
    p_vec = lax.dynamic_index_in_dim(p_all, at_rep, 0, keepdims=False)
    scale_in = coef * jnp.sqrt(jnp.sum(left_one * left_one) / p_norm)
    scale_out = coef * jnp.sqrt(sums[-1] / q_norm)

    raw = times(jnp.concatenate([tok, probe], 0), full_in)
    raw_z = raw[:n]
    e_one = scale_in * raw[n:]
    tanh_z = jnp.tanh(scale_in * raw_z + bias_all)
    deriv = 1.0 - tanh_z * tanh_z
    act = tanh_z.astype(BF16)
    r_one = (e_one * deriv).astype(BF16)
    j_part = scale_out * times(r_one, full_out)
    j_one = gather_rows(scatter_sum(j_part, planes, core).astype(BF16), core)
    branch = scatter_sum(scale_out * times(act, full_out), planes, core)
    output = lax.all_gather(
        (tok_own.astype(F32) + branch).astype(BF16), ("x", "c"), axis=0, tiled=True
    )
    backs = contract_cols(jnp.concatenate([probe, cot], 0), full_out)
    raw_b = backs[:n]
    raw_c = backs[n:]
    hd = deriv * (scale_out * raw_b)
    h_round = hd.astype(BF16)

    e_two = scale_in * times(j_one, full_in)
    r_two = (e_two * deriv).astype(BF16)
    j_part = scale_out * times(r_two, full_out)
    j_two = gather_rows(scatter_sum(j_part, planes, core).astype(BF16), core)
    e_three = scale_in * times(j_two, full_in)

    a_vec = e_one - e_two + e_three
    g_round = (a_vec * deriv).astype(BF16)
    second = -2.0 * tanh_z * deriv
    dz_vec = scale_out * raw_c * deriv - a_vec * (scale_out * raw_b) * second
    dz_round = dz_vec.astype(BF16)
    w_vec = (probe.astype(F32) - j_one.astype(F32) + j_two.astype(F32)).astype(BF16)

    terms = jnp.sum((e_one - e_two / 2.0 + e_three / 3.0) * hd, axis=1)
    inner_one = jnp.sum(dz_round.astype(F32) * raw_z - h_round.astype(F32) * (a_vec / scale_in))
    inner_two = jnp.sum(act.astype(F32) * raw_c - g_round.astype(F32) * raw_b)
    t_slots = jnp.where(
        jnp.arange(4)[:, None] == at_y * 2 + at_x, terms[None, :], 0.0
    ).reshape(-1)
    tail = lax.psum(jnp.concatenate([t_slots, inner_one[None], inner_two[None]]), EVERY)
    inner_one = tail[-2]
    inner_two = tail[-1]
    logdet = lax.dynamic_slice(
        tail[:-2].reshape(2, 2, 2, planes, quarter),
        (at_y, 0, 0, at_z, 0),
        (1, 2, 2, 1, quarter),
    ).reshape(count)

    grad_one = contract_rows(
        jnp.concatenate([tok, w_vec], 0), jnp.concatenate([dz_round, -h_round], 0)
    ).astype(BF16)
    grad_one = grad_one.reshape(planes, 2, rows_in, 2, piece).transpose(3, 1, 0, 2, 4)
    grad_one = lax.psum_scatter(
        grad_one.reshape(4 * planes * rows_in, piece), ("x", "y"), scatter_dimension=0, tiled=True
    )
    grad_one = lax.all_to_all(grad_one, "z", 0, 1, tiled=True).astype(F32)

    grad_two = contract_rows(
        jnp.concatenate([act, g_round], 0), jnp.concatenate([cot, -probe], 0)
    ).astype(BF16)
    grad_two = lax.psum_scatter(grad_two, ("x", "y"), scatter_dimension=0, tiled=True).astype(F32)

    dx = scatter_sum(scale_in * contract_cols(dz_round, full_in), planes, core)
    dx_all = lax.all_gather(dx.astype(BF16), ("x", "c"), axis=0, tiled=True)
    grad_tokens = cotangent.astype(F32) + dx_all.astype(F32)

    grad_in = scale_in * (grad_one - inner_one * slice_one[:, None] * p_vec[None, :] / p_norm)
    grad_out = scale_out * (grad_two - inner_two * slice_two[:, None] * q_vec[None, :] / q_norm)
    return (output, logdet, grad_tokens, grad_in, grad_out)


def solution(mesh):
    fine = Mesh(
        mesh.devices.reshape(mesh.shape["dp"] // 2, 2, mesh.shape["rep"] // 2, 2), EVERY
    )
    dp, rep = ("z", "y"), ("x", "c")
    placed = (
        P(dp, None),
        P(dp, None),
        P(dp),
        P(dp, rep),
        P(rep),
        P(rep + dp, None),
        P(),
        P(rep),
    )
    return jax.shard_map(
        on_device,
        mesh=fine,
        in_specs=placed,
        out_specs=(P(dp, None), P(dp), P(dp, None), P(dp, rep), P(rep + dp, None)),
        check_vma=False,
    )
```

```python
import jax
import jax.numpy as jnp
from jax import lax
from jax.sharding import Mesh
from jax.sharding import PartitionSpec as P

F32 = jnp.float32
BF16 = jnp.bfloat16
EVERY = ("z", "y", "x", "c")
SWAP = [(0, 1), (1, 0)]


def probe_signs(seeds, width):
    columns = jnp.arange(width, dtype=jnp.int32)
    mixed = seeds[:, None] * 747796405 + columns[None, :] * 1640531527
    mixed = mixed ^ lax.shift_right_logical(mixed, jnp.full_like(mixed, 16))
    mixed = mixed * 668265261
    mixed = mixed ^ lax.shift_right_logical(mixed, jnp.full_like(mixed, 15))
    lowbit = jnp.bitwise_and(lax.shift_right_logical(mixed, jnp.full_like(mixed, 7)), 1)
    return (1 - 2 * lowbit).astype(F32).astype(BF16)


def times(left, right):
    return jnp.dot(left, right, preferred_element_type=F32)


def contract_rows(left, right):
    return lax.dot_general(left, right, (((0,), (0,)), ((), ())), preferred_element_type=F32)


def contract_cols(left, right):
    return lax.dot_general(left, right, (((1,), (1,)), ((), ())), preferred_element_type=F32)


def in_order(own, other, index):
    first = jnp.where(index == 0, own, other)
    second = jnp.where(index == 0, other, own)
    return jnp.concatenate([first, second], 0)


def sum_over(values, names):
    for name in names:
        size, step = lax.axis_size(name), 1
        while step < size:
            pairs = [(place, place ^ step) for place in range(size)]
            values = values + lax.ppermute(values, name, pairs)
            step *= 2
    return values


def spread(block, after=None):
    half = block.shape[0] // 2
    x_low = lax.ppermute(block[half:], "x", SWAP)
    y_top = lax.ppermute(block[:half], "y", SWAP)
    x_top = lax.ppermute(block[:half], "x", SWAP)
    y_low = lax.ppermute(block[half:], "y", SWAP)
    if after is not None:
        x_low, y_top, _ = lax.optimization_barrier((x_low, y_top, after))
    far_top = lax.ppermute(y_top, "x", SWAP)
    far_low = lax.ppermute(x_low, "y", SWAP)
    stack = lambda top, low: jnp.concatenate([top, low], 0)
    return stack(x_top, x_low), stack(y_top, y_low), stack(far_top, far_low)


def collect(own, to_x, to_y, across):
    half = own.shape[0] // 2
    across = across.astype(BF16)
    across_x = lax.ppermute(across[:half], "x", SWAP)
    across_y = lax.ppermute(across[half:], "y", SWAP)
    x_top = lax.ppermute(to_x[:half].astype(BF16), "x", SWAP)
    y_low = lax.ppermute(to_y[half:].astype(BF16), "y", SWAP)
    x_low = (to_x[half:] + across_y.astype(F32)).astype(BF16)
    y_top = (to_y[:half] + across_x.astype(F32)).astype(BF16)
    x_low = lax.ppermute(x_low, "x", SWAP)
    y_top = lax.ppermute(y_top, "y", SWAP)
    top = own[:half] + x_top.astype(F32) + y_top.astype(F32)
    low = own[half:] + x_low.astype(F32) + y_low.astype(F32)
    return jnp.concatenate([top, low], 0)


def scatter_sum(part, planes, core):
    half = part.shape[0] // 2
    keep = lax.dynamic_slice_in_dim(part, core * half, half, 0)
    give = lax.dynamic_slice_in_dim(part, (1 - core) * half, half, 0).astype(BF16)
    pair = (keep + lax.ppermute(give, "c", SWAP).astype(F32)).astype(BF16)
    got = lax.all_to_all(pair, "z", 0, 0, tiled=True)
    return jnp.sum(got.reshape(planes, half // planes, -1).astype(F32), 0)


def gather_rows(quarter, core):
    half = lax.all_gather(quarter, "z", axis=0, tiled=True)
    return in_order(half, lax.ppermute(half, "c", SWAP), core)


def on_device(tokens, cotangent, probe_seed, w_in, bias, w_out, left_in, left_out):
    coef = 0.9
    planes = lax.axis_size("z")
    at_z, at_y, at_x, core = (lax.axis_index(name) for name in EVERY)
    count, width = tokens.shape
    rows_in, hid_rep = w_in.shape
    rows_out = w_out.shape[0]
    piece = hid_rep // planes
    quarter = count // 4
    at_dp = at_z * 2 + at_y
    at_rep = at_x * 2 + core

    in_z = lax.all_to_all(w_in, "z", 1, 0, tiled=True)
    in_x, in_y, in_d = spread(in_z)
    out_x, out_y, out_d = spread(w_out, in_x)
    full_out = jnp.concatenate([in_order(w_out, out_y, at_y), in_order(out_x, out_d, at_y)], 0)

    def join_rows(own, other):
        first = jnp.where(at_y == 0, own, other).reshape(planes, 1, rows_in, piece)
        second = jnp.where(at_y == 0, other, own).reshape(planes, 1, rows_in, piece)
        return jnp.concatenate([first, second], 1).reshape(width, piece)

    full_in = jnp.concatenate([join_rows(in_z, in_y), join_rows(in_x, in_d)], 1)

    def own_quarter(array):
        return lax.dynamic_slice_in_dim(array, at_rep * quarter, quarter, 0)

    tok_own = own_quarter(tokens)
    pair = jnp.stack([tok_own, own_quarter(cotangent)])
    pair = lax.all_gather(pair, "z", axis=1)
    tok = in_order(pair[0], lax.ppermute(pair[0], "c", SWAP), core).reshape(-1, width)
    cot = in_order(pair[1], lax.ppermute(pair[1], "c", SWAP), core).reshape(-1, width)
    seeds = lax.all_gather(own_quarter(probe_seed), ("c", "z"), axis=0, tiled=True)
    probe = probe_signs(seeds, width)
    n = tok.shape[0]
    bias_own = lax.dynamic_slice_in_dim(bias, at_z * piece, piece, 0)
    bias_all = jnp.concatenate([bias_own, lax.ppermute(bias_own, "x", SWAP)])

    left_one = left_in.astype(F32)
    slice_one = lax.dynamic_slice_in_dim(left_in, at_dp * rows_in, rows_in, 0)
    slice_two = lax.dynamic_slice_in_dim(left_out, at_dp * rows_out, rows_out, 0)
    p_part = times(slice_one, w_in)
    q_part = times(slice_two, w_out)
    slice_one = slice_one.astype(F32)
    slice_two = slice_two.astype(F32)
    sums = sum_over(
        jnp.concatenate([p_part, q_part, jnp.sum(slice_two * slice_two)[None]]), ("z", "y")
    )
    p_vec = sums[:hid_rep]
    sums = sum_over(jnp.concatenate([sums[hid_rep:], jnp.sum(p_vec * p_vec)[None]]), ("c", "x"))
    q_vec = sums[:width]
    p_norm = sums[-1]
    q_norm = jnp.sum(q_vec * q_vec)
    scale_in = coef * jnp.sqrt(jnp.sum(left_one * left_one) / p_norm)
    scale_out = coef * jnp.sqrt(sums[-2] / q_norm)

    raw = times(jnp.concatenate([tok, probe], 0), full_in)
    raw_z = raw[:n]
    e_one = scale_in * raw[n:]
    tanh_z = jnp.tanh(scale_in * raw_z + bias_all)
    deriv = 1.0 - tanh_z * tanh_z
    act = tanh_z.astype(BF16)
    r_one = (e_one * deriv).astype(BF16)
    j_part = scale_out * times(r_one, full_out)
    j_one = gather_rows(scatter_sum(j_part, planes, core).astype(BF16), core)
    branch = scatter_sum(scale_out * times(act, full_out), planes, core)
    output = lax.all_gather(
        (tok_own.astype(F32) + branch).astype(BF16), ("x", "c"), axis=0, tiled=True
    )
    backs = contract_cols(jnp.concatenate([probe, cot], 0), full_out)
    raw_b = backs[:n]
    raw_c = backs[n:]
    hd = deriv * (scale_out * raw_b)
    h_round = hd.astype(BF16)

    e_two = scale_in * times(j_one, full_in)
    r_two = (e_two * deriv).astype(BF16)
    j_part = scale_out * times(r_two, full_out)
    j_two = gather_rows(scatter_sum(j_part, planes, core).astype(BF16), core)
    e_three = scale_in * times(j_two, full_in)

    a_vec = e_one - e_two + e_three
    g_round = (a_vec * deriv).astype(BF16)
    second = -2.0 * tanh_z * deriv
    dz_vec = scale_out * raw_c * deriv - a_vec * (scale_out * raw_b) * second
    dz_round = dz_vec.astype(BF16)
    w_vec = (probe.astype(F32) - j_one.astype(F32) + j_two.astype(F32)).astype(BF16)

    terms = jnp.sum((e_one - e_two / 2.0 + e_three / 3.0) * hd, axis=1)
    inner_one = jnp.sum(dz_round.astype(F32) * raw_z - h_round.astype(F32) * (a_vec / scale_in))
    inner_two = jnp.sum(act.astype(F32) * raw_c - g_round.astype(F32) * raw_b)
    tail = sum_over(jnp.concatenate([terms, inner_one[None], inner_two[None]]), ("c", "z"))
    terms = lax.dynamic_index_in_dim(tail[:n].reshape(2, planes, quarter), at_z, 1, keepdims=False)
    tail = jnp.concatenate([tail[n:], terms.reshape(-1)])
    tail_x = lax.ppermute(tail, "x", SWAP)
    logdet = in_order(tail[2:], tail_x[2:], at_x)
    inner = sum_over(tail[:2] + tail_x[:2], ("y",))
    inner_one = inner[0]
    inner_two = inner[1]

    left_grad = jnp.concatenate([tok, w_vec], 0).reshape(2 * n, planes, 2, rows_in)
    right_grad = jnp.concatenate([dz_round, -h_round], 0)

    def block_one(y_index, x_other):
        left = lax.dynamic_index_in_dim(left_grad, y_index, 2, keepdims=False)
        right = right_grad[:, x_other * piece : (x_other + 1) * piece]
        return contract_rows(left.reshape(2 * n, planes * rows_in), right)

    across = block_one(1 - at_y, 1)
    grad_one = collect(block_one(at_y, 0), block_one(at_y, 1), block_one(1 - at_y, 0), across)
    grad_one = lax.all_to_all(grad_one.astype(BF16), "z", 0, 1, tiled=True).astype(F32)

    left_two = jnp.concatenate([act, g_round], 0).reshape(2 * n, 2, 2, rows_out)
    right_two = jnp.concatenate([cot, -probe], 0)

    def block_two(y_index, x_other):
        left = lax.dynamic_index_in_dim(left_two[:, x_other], y_index, 1, keepdims=False)
        return contract_rows(left, right_two)

    across = block_two(1 - at_y, 1)
    grad_two = collect(block_two(at_y, 0), block_two(at_y, 1), block_two(1 - at_y, 0), across)

    dx = scatter_sum(scale_in * contract_cols(dz_round, full_in), planes, core)
    dx_all = lax.all_gather(dx.astype(BF16), ("x", "c"), axis=0, tiled=True)
    grad_tokens = cotangent.astype(F32) + dx_all.astype(F32)

    grad_in = scale_in * (grad_one - inner_one * slice_one[:, None] * p_vec[None, :] / p_norm)
    grad_out = scale_out * (grad_two - inner_two * slice_two[:, None] * q_vec[None, :] / q_norm)
    return (output, logdet, grad_tokens, grad_in, grad_out)


def solution(mesh):
    fine = Mesh(
        mesh.devices.reshape(mesh.shape["dp"] // 2, 2, mesh.shape["rep"] // 2, 2), EVERY
    )
    dp, rep = ("z", "y"), ("x", "c")
    placed = (
        P(dp, None),
        P(dp, None),
        P(dp),
        P(dp, rep),
        P(rep),
        P(rep + dp, None),
        P(),
        P(rep),
    )
    return jax.shard_map(
        on_device,
        mesh=fine,
        in_specs=placed,
        out_specs=(P(dp, None), P(dp), P(dp, None), P(dp, rep), P(rep + dp, None)),
        check_vma=False,
    )
```

```python
import jax
import jax.numpy as jnp
from jax import lax
from jax.sharding import Mesh
from jax.sharding import PartitionSpec as P

F32 = jnp.float32
BF16 = jnp.bfloat16
EVERY = ("z", "y", "x", "c")
SWAP = [(0, 1), (1, 0)]


def probe_signs(seeds, width):
    columns = jnp.arange(width, dtype=jnp.int32)
    mixed = seeds[:, None] * 747796405 + columns[None, :] * 1640531527
    mixed = mixed ^ lax.shift_right_logical(mixed, jnp.full_like(mixed, 16))
    mixed = mixed * 668265261
    mixed = mixed ^ lax.shift_right_logical(mixed, jnp.full_like(mixed, 15))
    lowbit = jnp.bitwise_and(lax.shift_right_logical(mixed, jnp.full_like(mixed, 7)), 1)
    return (1 - 2 * lowbit).astype(F32).astype(BF16)


def times(left, right):
    return jnp.dot(left, right, preferred_element_type=F32)


def contract_rows(left, right):
    return lax.dot_general(left, right, (((0,), (0,)), ((), ())), preferred_element_type=F32)


def contract_cols(left, right):
    return lax.dot_general(left, right, (((1,), (1,)), ((), ())), preferred_element_type=F32)


def in_order(own, other, index):
    first = jnp.where(index == 0, own, other)
    second = jnp.where(index == 0, other, own)
    return jnp.concatenate([first, second], 0)


def sum_over(values, names):
    for name in names:
        size, step = lax.axis_size(name), 1
        while step < size:
            pairs = [(place, place ^ step) for place in range(size)]
            values = values + lax.ppermute(values, name, pairs)
            step *= 2
    return values


def spread(block):
    half = block.shape[0] // 2
    x_low = lax.ppermute(block[half:], "x", SWAP)
    y_top = lax.ppermute(block[:half], "y", SWAP)
    x_top = lax.ppermute(block[:half], "x", SWAP)
    y_low = lax.ppermute(block[half:], "y", SWAP)
    far_top = lax.ppermute(y_top, "x", SWAP)
    far_low = lax.ppermute(x_low, "y", SWAP)
    stack = lambda top, low: jnp.concatenate([top, low], 0)
    return stack(x_top, x_low), stack(y_top, y_low), stack(far_top, far_low)


def exchange(to_x, to_y, across):
    return (
        lax.ppermute(to_x, "x", SWAP),
        lax.ppermute(to_y, "y", SWAP),
        lax.ppermute(across, ("y", "x"), [(place, 3 - place) for place in range(4)]),
    )


def scatter_sum(part, planes, core):
    half = part.shape[0] // 2
    keep = lax.dynamic_slice_in_dim(part, core * half, half, 0)
    give = lax.dynamic_slice_in_dim(part, (1 - core) * half, half, 0).astype(BF16)
    pair = (keep + lax.ppermute(give, "c", SWAP).astype(F32)).astype(BF16)
    got = lax.all_to_all(pair, "z", 0, 0, tiled=True)
    return jnp.sum(got.reshape(planes, half // planes, -1).astype(F32), 0)


def gather_rows(quarter, core):
    half = lax.all_gather(quarter, "z", axis=0, tiled=True)
    return in_order(half, lax.ppermute(half, "c", SWAP), core)


def on_device(tokens, cotangent, probe_seed, w_in, bias, w_out, left_in, left_out):
    coef = 0.9
    planes = lax.axis_size("z")
    at_z, at_y, at_x, core = (lax.axis_index(name) for name in EVERY)
    count, width = tokens.shape
    rows_in, hid_rep = w_in.shape
    rows_out = w_out.shape[0]
    piece = hid_rep // planes
    quarter = count // 4
    at_dp = at_z * 2 + at_y
    at_rep = at_x * 2 + core

    in_z = lax.all_to_all(w_in, "z", 1, 0, tiled=True)
    out_x, out_y, out_d = spread(w_out)

    def own_quarter(array):
        return lax.dynamic_slice_in_dim(array, at_rep * quarter, quarter, 0)

    tok_own = own_quarter(tokens)
    pair = jnp.stack([tok_own, own_quarter(cotangent)])
    slice_one = lax.dynamic_slice_in_dim(left_in, at_dp * rows_in, rows_in, 0)
    slice_two = lax.dynamic_slice_in_dim(left_out, at_dp * rows_out, rows_out, 0)
    seeds = jnp.where(
        jnp.arange(2 * planes)[:, None] == core * planes + at_z, own_quarter(probe_seed)[None, :], 0
    ).reshape(-1)
    in_z, pair, slice_one, slice_two, seeds = lax.optimization_barrier(
        (in_z, pair, slice_one, slice_two, seeds)
    )
    in_x, in_y, in_d = spread(in_z)
    full_out = jnp.concatenate([in_order(w_out, out_y, at_y), in_order(out_x, out_d, at_y)], 0)

    def join_rows(own, other):
        first = jnp.where(at_y == 0, own, other).reshape(planes, 1, rows_in, piece)
        second = jnp.where(at_y == 0, other, own).reshape(planes, 1, rows_in, piece)
        return jnp.concatenate([first, second], 1).reshape(width, piece)

    full_in = jnp.concatenate([join_rows(in_z, in_y), join_rows(in_x, in_d)], 1)

    pair = lax.all_gather(pair, "z", axis=1)
    tok = in_order(pair[0], lax.ppermute(pair[0], "c", SWAP), core).reshape(-1, width)
    cot = in_order(pair[1], lax.ppermute(pair[1], "c", SWAP), core).reshape(-1, width)
    seeds = sum_over(seeds, ("c", "z"))
    probe = probe_signs(seeds, width)
    n = tok.shape[0]
    bias_own = lax.dynamic_slice_in_dim(bias, at_z * piece, piece, 0)
    bias_all = jnp.concatenate([bias_own, lax.ppermute(bias_own, "x", SWAP)])

    left_one = left_in.astype(F32)
    p_part = times(slice_one, w_in)
    q_part = times(slice_two, w_out)
    slice_one = slice_one.astype(F32)
    slice_two = slice_two.astype(F32)
    sums = sum_over(
        jnp.concatenate([p_part, q_part, jnp.sum(slice_two * slice_two)[None]]), ("z", "y")
    )
    p_vec = sums[:hid_rep]
    sums = sum_over(jnp.concatenate([sums[hid_rep:], jnp.sum(p_vec * p_vec)[None]]), ("c", "x"))
    q_vec = sums[:width]
    p_norm = sums[-1]
    q_norm = jnp.sum(q_vec * q_vec)
    scale_in = coef * jnp.sqrt(jnp.sum(left_one * left_one) / p_norm)
    scale_out = coef * jnp.sqrt(sums[-2] / q_norm)

    raw = times(jnp.concatenate([tok, probe], 0), full_in)
    raw_z = raw[:n]
    e_one = scale_in * raw[n:]
    tanh_z = jnp.tanh(scale_in * raw_z + bias_all)
    deriv = 1.0 - tanh_z * tanh_z
    act = tanh_z.astype(BF16)
    r_one = (e_one * deriv).astype(BF16)

    def own_units(array, y_index, x_other):
        start = (2 * x_other + y_index) * rows_out
        return lax.dynamic_slice_in_dim(array, start, rows_out, 1)

    def exchange_units(array):
        parts = exchange(
            own_units(array, at_y, 1), own_units(array, 1 - at_y, 0), own_units(array, 1 - at_y, 1)
        )
        return jnp.concatenate([own_units(array, at_y, 0), *parts], 0)

    factors = n <= 4 * rows_out
    if factors:
        cot_late, seeds_late, act_late, r_one = lax.optimization_barrier((cot, seeds, act, r_one))
        act_units = exchange_units(act_late)
        seeds_x = lax.ppermute(seeds_late, "x", SWAP)
        seeds_y = lax.ppermute(seeds_late, "y", SWAP)
        seeds_d = lax.ppermute(seeds_x, "y", SWAP)
        cot_rows = jnp.concatenate([cot_late, *spread(cot_late)], 0)

    j_part = scale_out * times(r_one, full_out)
    j_one = gather_rows(scatter_sum(j_part, planes, core).astype(BF16), core)
    branch = scatter_sum(scale_out * times(act, full_out), planes, core)
    output = lax.all_gather(
        (tok_own.astype(F32) + branch).astype(BF16), ("x", "c"), axis=0, tiled=True
    )
    backs = contract_cols(jnp.concatenate([probe, cot], 0), full_out)
    raw_b = backs[:n]
    raw_c = backs[n:]
    hd = deriv * (scale_out * raw_b)
    h_round = hd.astype(BF16)

    e_two = scale_in * times(j_one, full_in)
    r_two = (e_two * deriv).astype(BF16)
    j_part = scale_out * times(r_two, full_out)
    j_two = gather_rows(scatter_sum(j_part, planes, core).astype(BF16), core)
    e_three = scale_in * times(j_two, full_in)

    a_vec = e_one - e_two + e_three
    g_round = (a_vec * deriv).astype(BF16)
    second = -2.0 * tanh_z * deriv
    dz_vec = scale_out * raw_c * deriv - a_vec * (scale_out * raw_b) * second
    dz_round = dz_vec.astype(BF16)
    w_vec = (probe.astype(F32) - j_one.astype(F32) + j_two.astype(F32)).astype(BF16)

    terms = jnp.sum((e_one - e_two / 2.0 + e_three / 3.0) * hd, axis=1)
    inner_one = jnp.sum(dz_round.astype(F32) * raw_z - h_round.astype(F32) * (a_vec / scale_in))
    inner_two = jnp.sum(act.astype(F32) * raw_c - g_round.astype(F32) * raw_b)
    tail = sum_over(jnp.concatenate([terms, inner_one[None], inner_two[None]]), ("c", "z"))
    terms = lax.dynamic_index_in_dim(tail[:n].reshape(2, planes, quarter), at_z, 1, keepdims=False)
    tail = jnp.concatenate([tail[n:], terms.reshape(-1)])
    tail_x = lax.ppermute(tail, "x", SWAP)
    logdet = in_order(tail[2:], tail_x[2:], at_x)
    inner = sum_over(tail[:2] + tail_x[:2], ("y",))
    inner_one = inner[0]
    inner_two = inner[1]

    left_grad = jnp.concatenate([tok, w_vec], 0)
    right_grad = jnp.concatenate([dz_round, -h_round], 0)
    right_cols = (right_grad[:, :piece], right_grad[:, piece:])

    def left_rows(y_index, low):
        starts = [(2 * plane + y_index) * rows_in for plane in range(planes)]
        starts = starts[planes // 2 :] if low else starts[: planes // 2]
        return jnp.concatenate(
            [lax.dynamic_slice_in_dim(left_grad, start, rows_in, 1) for start in starts], 1
        )

    near_top, near_low = left_rows(at_y, 0), left_rows(at_y, 1)
    over_top, over_low = left_rows(1 - at_y, 0), left_rows(1 - at_y, 1)
    across_x = lax.ppermute(contract_rows(over_top, right_cols[1]).astype(BF16), "x", SWAP)
    across_y = lax.ppermute(contract_rows(over_low, right_cols[1]).astype(BF16), "y", SWAP)
    x_top = lax.ppermute(contract_rows(near_top, right_cols[1]).astype(BF16), "x", SWAP)
    y_low = lax.ppermute(contract_rows(over_low, right_cols[0]).astype(BF16), "y", SWAP)
    x_low = contract_rows(near_low, right_cols[1]) + across_y.astype(F32)
    y_top = contract_rows(over_top, right_cols[0]) + across_x.astype(F32)
    x_low = lax.ppermute(x_low.astype(BF16), "x", SWAP)
    y_top = lax.ppermute(y_top.astype(BF16), "y", SWAP)
    top = contract_rows(near_top, right_cols[0]) + x_top.astype(F32) + y_top.astype(F32)
    low = contract_rows(near_low, right_cols[0]) + x_low.astype(F32) + y_low.astype(F32)
    grad_one = jnp.concatenate([top.astype(BF16), low.astype(BF16)], 0)
    grad_one = lax.all_to_all(grad_one, "z", 0, 1, tiled=True).astype(F32)

    dz_late, g_late, _ = lax.optimization_barrier((dz_round, g_round, across_x))
    if factors:
        probes = [probe_signs(v, width) for v in (seeds_x, seeds_y, seeds_d)]
        grad_two = contract_rows(act_units, cot_rows)
        grad_two = grad_two - contract_rows(
            exchange_units(g_late), jnp.concatenate([probe, *probes], 0)
        )
    else:

        def block_two(y_index, x_other):
            grad = contract_rows(own_units(act, y_index, x_other), cot)
            return grad - contract_rows(own_units(g_late, y_index, x_other), probe)

        parts = exchange(
            block_two(at_y, 1).astype(BF16),
            block_two(1 - at_y, 0).astype(BF16),
            block_two(1 - at_y, 1).astype(BF16),
        )
        grad_two = block_two(at_y, 0) + sum(part.astype(F32) for part in parts)

    dx = scatter_sum(scale_in * contract_cols(dz_late, full_in), planes, core)
    dx_all = lax.all_gather(dx.astype(BF16), ("x", "c"), axis=0, tiled=True)
    grad_tokens = cotangent.astype(F32) + dx_all.astype(F32)

    grad_in = scale_in * (grad_one - inner_one * slice_one[:, None] * p_vec[None, :] / p_norm)
    grad_out = scale_out * (grad_two - inner_two * slice_two[:, None] * q_vec[None, :] / q_norm)
    return (output, logdet, grad_tokens, grad_in, grad_out)


def solution(mesh):
    fine = Mesh(
        mesh.devices.reshape(mesh.shape["dp"] // 2, 2, mesh.shape["rep"] // 2, 2), EVERY
    )
    dp, rep = ("z", "y"), ("x", "c")
    placed = (
        P(dp, None),
        P(dp, None),
        P(dp),
        P(dp, rep),
        P(rep),
        P(rep + dp, None),
        P(),
        P(rep),
    )
    return jax.shard_map(
        on_device,
        mesh=fine,
        in_specs=placed,
        out_specs=(P(dp, None), P(dp), P(dp, None), P(dp, rep), P(rep + dp, None)),
        check_vma=False,
    )
```

```python
import jax
import jax.numpy as jnp
from jax import lax
from jax.sharding import Mesh
from jax.sharding import PartitionSpec as P

F32 = jnp.float32
BF16 = jnp.bfloat16
EVERY = ("z", "y", "x", "c")
SWAP = [(0, 1), (1, 0)]


def probe_signs(seeds, width):
    columns = jnp.arange(width, dtype=jnp.int32)
    mixed = seeds[:, None] * 747796405 + columns[None, :] * 1640531527
    mixed = mixed ^ lax.shift_right_logical(mixed, jnp.full_like(mixed, 16))
    mixed = mixed * 668265261
    mixed = mixed ^ lax.shift_right_logical(mixed, jnp.full_like(mixed, 15))
    lowbit = jnp.bitwise_and(lax.shift_right_logical(mixed, jnp.full_like(mixed, 7)), 1)
    return (1 - 2 * lowbit).astype(F32).astype(BF16)


def times(left, right):
    return jnp.dot(left, right, preferred_element_type=F32)


def contract_rows(left, right):
    return lax.dot_general(left, right, (((0,), (0,)), ((), ())), preferred_element_type=F32)


def contract_cols(left, right):
    return lax.dot_general(left, right, (((1,), (1,)), ((), ())), preferred_element_type=F32)


def in_order(own, other, index):
    first = jnp.where(index == 0, own, other)
    second = jnp.where(index == 0, other, own)
    return jnp.concatenate([first, second], 0)


def sum_over(values, names):
    for name in names:
        size, step = lax.axis_size(name), 1
        while step < size:
            pairs = [(place, place ^ step) for place in range(size)]
            values = values + lax.ppermute(values, name, pairs)
            step *= 2
    return values


def spread(block):
    half = block.shape[0] // 2
    x_low = lax.ppermute(block[half:], "x", SWAP)
    y_top = lax.ppermute(block[:half], "y", SWAP)
    x_top = lax.ppermute(block[:half], "x", SWAP)
    y_low = lax.ppermute(block[half:], "y", SWAP)
    far_top = lax.ppermute(y_top, "x", SWAP)
    far_low = lax.ppermute(x_low, "y", SWAP)
    stack = lambda top, low: jnp.concatenate([top, low], 0)
    return stack(x_top, x_low), stack(y_top, y_low), stack(far_top, far_low)


def exchange(to_x, to_y, across):
    return (
        lax.ppermute(to_x, "x", SWAP),
        lax.ppermute(to_y, "y", SWAP),
        lax.ppermute(across, ("y", "x"), [(place, 3 - place) for place in range(4)]),
    )


def fold_cores(part):
    half = part.shape[0] // 2
    got = lax.ppermute(part[half:].astype(BF16), "c", SWAP)
    return (part[:half] + got.astype(F32)).astype(BF16)


def sum_planes(rows):
    got = lax.all_to_all(rows, "z", 0, 0, tiled=True)
    planes = lax.axis_size("z")
    return jnp.sum(got.reshape(planes, rows.shape[0] // planes, -1).astype(F32), 0)


def with_other_core(half):
    return jnp.concatenate([half, lax.ppermute(half, "c", SWAP)], 0)


def gather_rows(quarter):
    return with_other_core(lax.all_gather(quarter, "z", axis=0, tiled=True))


def exchange_shared(to_x, to_y, across):
    half = to_x.shape[0] // 2
    parts = exchange(to_x[:half], to_y[:half], across[:half])
    return tuple(with_other_core(part) for part in parts)


def behind(values, *before):
    return lax.optimization_barrier((values, before))[0]


def on_device(tokens, cotangent, probe_seed, w_in, bias, w_out, left_in, left_out):
    coef = 0.9
    planes = lax.axis_size("z")
    at_z, at_y, at_x, core = (lax.axis_index(name) for name in EVERY)
    count, width = tokens.shape
    rows_in, hid_rep = w_in.shape
    rows_out = w_out.shape[0]
    piece = hid_rep // planes
    quarter = count // 4
    at_dp = at_z * 2 + at_y
    at_rep = at_x * 2 + core

    def own_quarter(array):
        return lax.dynamic_slice_in_dim(array, at_rep * quarter, quarter, 0)

    def rows_of(array, y_index):
        starts = [(2 * plane + y_index) * rows_in for plane in range(planes)]
        return jnp.concatenate(
            [lax.dynamic_slice_in_dim(array, start, rows_in, 1) for start in starts], 1
        )

    def units_of(array, y_index, x_other):
        start = (2 * x_other + y_index) * rows_out
        return lax.dynamic_slice_in_dim(array, start, rows_out, 1)

    in_z = lax.all_to_all(w_in, "z", 1, 0, tiled=True)
    out_x, out_y, out_d = spread(w_out)
    full_out = jnp.concatenate([in_order(w_out, out_y, at_y), in_order(out_x, out_d, at_y)], 0)

    def join_rows(own, other):
        first = jnp.where(at_y == 0, own, other).reshape(planes, 1, rows_in, piece)
        second = jnp.where(at_y == 0, other, own).reshape(planes, 1, rows_in, piece)
        return jnp.concatenate([first, second], 1).reshape(width, piece)

    in_x, in_y, in_d = spread(in_z)
    full_in = jnp.concatenate([join_rows(in_z, in_y), join_rows(in_x, in_d)], 1)

    tok_own = own_quarter(tokens)
    pair = behind(jnp.stack([tok_own, own_quarter(cotangent)]), in_z)
    pair = lax.all_gather(pair, "z", axis=1)
    tok = with_other_core(pair[0].reshape(-1, width))
    cot = with_other_core(pair[1].reshape(-1, width))
    n = tok.shape[0]
    seeds = jnp.where(
        jnp.arange(planes)[:, None] == at_z, own_quarter(probe_seed)[None, :], 0
    ).reshape(-1)
    seeds = with_other_core(sum_over(seeds, ("z",)))
    probe = probe_signs(seeds, width)
    bias_own = lax.dynamic_slice_in_dim(bias, at_z * piece, piece, 0)
    bias_all = jnp.concatenate([bias_own, lax.ppermute(bias_own, "x", SWAP)])

    left_one = left_in.astype(F32)
    slice_one = lax.dynamic_slice_in_dim(left_in, at_dp * rows_in, rows_in, 0)
    slice_two = lax.dynamic_slice_in_dim(left_out, at_dp * rows_out, rows_out, 0)
    p_part = times(slice_one, w_in)
    q_part = times(slice_two, w_out)
    slice_one = slice_one.astype(F32)
    slice_two = slice_two.astype(F32)
    sums = sum_over(
        jnp.concatenate([p_part, q_part, jnp.sum(slice_two * slice_two)[None]]), ("z", "y")
    )
    p_vec = sums[:hid_rep]
    sums = sum_over(jnp.concatenate([sums[hid_rep:], jnp.sum(p_vec * p_vec)[None]]), ("c", "x"))
    q_vec = sums[:width]
    p_norm = sums[-1]
    q_norm = jnp.sum(q_vec * q_vec)
    scale_in = coef * jnp.sqrt(jnp.sum(left_one * left_one) / p_norm)
    scale_out = coef * jnp.sqrt(sums[-2] / q_norm)

    raw = times(jnp.concatenate([tok, probe], 0), full_in)
    raw_z = raw[:n]
    e_one = scale_in * raw[n:]
    tanh_z = jnp.tanh(scale_in * raw_z + bias_all)
    deriv = 1.0 - tanh_z * tanh_z
    act = tanh_z.astype(BF16)
    r_one = (e_one * deriv).astype(BF16)
    j_pair = fold_cores(scale_out * times(r_one, full_out))
    j_one = gather_rows(sum_planes(j_pair).astype(BF16))

    factors = n <= 4 * rows_out
    tok_late, cot_late, seeds_late, probe_late = behind((tok, cot, seeds, probe), j_pair)
    if factors:
        tok_rows = exchange_shared(
            rows_of(tok_late, at_y), rows_of(tok_late, 1 - at_y), rows_of(tok_late, 1 - at_y)
        )
        cot_rows = exchange_shared(cot_late, cot_late, cot_late)
    backs = contract_cols(jnp.concatenate([probe_late, cot_late], 0), full_out)
    raw_b = backs[:n]
    raw_c = backs[n:]
    hd = deriv * (scale_out * raw_b)
    h_round = hd.astype(BF16)

    e_two = scale_in * times(j_one, full_in)
    r_two = (e_two * deriv).astype(BF16)
    j_pair = fold_cores(scale_out * times(r_two, full_out))
    j_two = gather_rows(sum_planes(j_pair).astype(BF16))

    act_late, h_late, seeds_late, probe_late = behind(
        (act, h_round, seeds_late, probe_late), j_pair
    )
    branch = fold_cores(scale_out * times(act_late, full_out))

    def exchange_units(array):
        return exchange(
            units_of(array, at_y, 1), units_of(array, 1 - at_y, 0), units_of(array, 1 - at_y, 1)
        )

    def exchange_pieces(array):
        return exchange(array[:, piece:], array[:, :piece], array[:, piece:])

    if factors:
        h_cols = exchange_pieces(h_late)
        act_units = exchange_units(act_late)
        seeds_x = lax.ppermute(seeds_late, "x", SWAP)
        seeds_y = lax.ppermute(seeds_late, "y", SWAP)
        seeds_d = lax.ppermute(seeds_x, "y", SWAP)
        grad_two = contract_rows(units_of(act_late, at_y, 0), cot)
        for left, right in zip(act_units, cot_rows):
            grad_two = grad_two + contract_rows(left, right)

    w_vec = (probe.astype(F32) - j_one.astype(F32) + j_two.astype(F32)).astype(BF16)
    if factors:
        w_rows = exchange_shared(
            rows_of(w_vec, at_y), rows_of(w_vec, 1 - at_y), rows_of(w_vec, 1 - at_y)
        )
    e_three = scale_in * times(j_two, full_in)
    a_vec = e_one - e_two + e_three
    second = -2.0 * tanh_z * deriv
    dz_vec = scale_out * raw_c * deriv - a_vec * (scale_out * raw_b) * second
    dz_round = dz_vec.astype(BF16)
    g_round = (a_vec * deriv).astype(BF16)

    def block_one(y_index, columns):
        grad = contract_rows(rows_of(tok, y_index), dz_round[:, columns])
        return grad - contract_rows(rows_of(w_vec, y_index), h_round[:, columns])

    own_cols, other_cols = slice(0, piece), slice(piece, 2 * piece)
    if factors:
        dz_cols = exchange_pieces(dz_round)
        started = dz_cols[1]
        grad_one = block_one(at_y, own_cols)
        for left, right in zip(w_rows, h_cols):
            grad_one = grad_one - contract_rows(left, right)
        for left, right in zip(tok_rows, dz_cols):
            grad_one = grad_one + contract_rows(left, right)
    else:
        parts = exchange(
            block_one(at_y, other_cols).astype(BF16),
            block_one(1 - at_y, own_cols).astype(BF16),
            block_one(1 - at_y, other_cols).astype(BF16),
        )
        started = parts[1]
        grad_one = block_one(at_y, own_cols) + sum(part.astype(F32) for part in parts)
    block = grad_one.astype(BF16)
    grad_one = lax.all_to_all(block, "z", 0, 1, tiled=True).astype(F32)

    g_late, a_late, e_late = behind((g_round, a_vec, e_three), started)
    if factors:
        g_units = exchange_units(g_late)
        grad_two = grad_two - contract_rows(units_of(g_late, at_y, 0), probe)
        for left, near in zip(g_units, (seeds_x, seeds_y, seeds_d)):
            grad_two = grad_two - contract_rows(left, probe_signs(near, width))
    else:

        def block_two(y_index, x_other):
            grad = contract_rows(units_of(act, y_index, x_other), cot)
            return grad - contract_rows(units_of(g_late, y_index, x_other), probe)

        parts = exchange(
            block_two(at_y, 1).astype(BF16),
            block_two(1 - at_y, 0).astype(BF16),
            block_two(1 - at_y, 1).astype(BF16),
        )
        grad_two = block_two(at_y, 0) + sum(part.astype(F32) for part in parts)

    dx = sum_planes(fold_cores(scale_in * contract_cols(dz_round, full_in))).astype(BF16)
    branch = sum_planes(behind(branch, j_two))
    output = (tok_own.astype(F32) + branch).astype(BF16)
    output, dx = behind((output, dx), block)
    output = lax.all_gather(output, ("x", "c"), axis=0, tiled=True)
    dx = lax.all_gather(dx, ("x", "c"), axis=0, tiled=True)
    grad_tokens = cotangent.astype(F32) + dx.astype(F32)

    terms = jnp.sum((e_one - e_two / 2.0 + e_late / 3.0) * hd, axis=1)
    inner_one = jnp.sum(dz_round.astype(F32) * raw_z - h_round.astype(F32) * (a_late / scale_in))
    inner_two = jnp.sum(act.astype(F32) * raw_c - g_late.astype(F32) * raw_b)
    inner = jnp.stack([inner_one, inner_two])
    tail = jnp.concatenate([terms, inner])
    got = lax.ppermute(tail, "c", SWAP)
    terms = terms + jnp.concatenate([got[n // 2 : n], got[: n // 2]])
    tail = sum_over(jnp.concatenate([terms, inner + got[n:]]), ("z",))
    terms = lax.dynamic_index_in_dim(tail[:n].reshape(2, planes, quarter), at_z, 1, keepdims=False)
    terms = in_order(terms[0], terms[1], core)
    tail = jnp.concatenate([tail[n:], terms])
    tail_x = lax.ppermute(tail, "x", SWAP)
    logdet = in_order(tail[2:], tail_x[2:], at_x)
    inner = sum_over(tail[:2] + tail_x[:2], ("y",))

    grad_in = scale_in * (grad_one - inner[0] * slice_one[:, None] * p_vec[None, :] / p_norm)
    grad_out = scale_out * (grad_two - inner[1] * slice_two[:, None] * q_vec[None, :] / q_norm)
    return (output, logdet, grad_tokens, grad_in, grad_out)


def solution(mesh):
    fine = Mesh(
        mesh.devices.reshape(mesh.shape["dp"] // 2, 2, mesh.shape["rep"] // 2, 2), EVERY
    )
    dp, rep = ("z", "y"), ("x", "c")
    placed = (
        P(dp, None),
        P(dp, None),
        P(dp),
        P(dp, rep),
        P(rep),
        P(rep + dp, None),
        P(),
        P(rep),
    )
    return jax.shard_map(
        on_device,
        mesh=fine,
        in_specs=placed,
        out_specs=(P(dp, None), P(dp), P(dp, None), P(dp, rep), P(rep + dp, None)),
        check_vma=False,
    )
```

```python
import jax
import jax.numpy as jnp
from jax import lax
from jax.sharding import Mesh
from jax.sharding import PartitionSpec as P

F32 = jnp.float32
BF16 = jnp.bfloat16
EVERY = ("z", "y", "x", "c")
SWAP = [(0, 1), (1, 0)]


def probe_signs(seeds, width):
    columns = jnp.arange(width, dtype=jnp.int32)
    mixed = seeds[:, None] * 747796405 + columns[None, :] * 1640531527
    mixed = mixed ^ lax.shift_right_logical(mixed, jnp.full_like(mixed, 16))
    mixed = mixed * 668265261
    mixed = mixed ^ lax.shift_right_logical(mixed, jnp.full_like(mixed, 15))
    lowbit = jnp.bitwise_and(lax.shift_right_logical(mixed, jnp.full_like(mixed, 7)), 1)
    return (1 - 2 * lowbit).astype(F32).astype(BF16)


def times(left, right):
    return jnp.dot(left, right, preferred_element_type=F32)


def contract_rows(left, right):
    return lax.dot_general(left, right, (((0,), (0,)), ((), ())), preferred_element_type=F32)


def contract_cols(left, right):
    return lax.dot_general(left, right, (((1,), (1,)), ((), ())), preferred_element_type=F32)


def in_order(own, other, index):
    first = jnp.where(index == 0, own, other)
    second = jnp.where(index == 0, other, own)
    return jnp.concatenate([first, second], 0)


def sum_over(values, names):
    for name in names:
        size, step = lax.axis_size(name), 1
        while step < size:
            pairs = [(place, place ^ step) for place in range(size)]
            values = values + lax.ppermute(values, name, pairs)
            step *= 2
    return values


tied = lax.optimization_barrier


def spread(block, *later):
    half = block.shape[0] // 2
    x_low = lax.ppermute(block[half:], "x", SWAP)
    y_top = lax.ppermute(block[:half], "y", SWAP)
    x_top = lax.ppermute(block[:half], "x", SWAP)
    y_low = lax.ppermute(block[half:], "y", SWAP)
    x_low, y_top, later = tied((x_low, y_top, later))
    far_top = lax.ppermute(y_top, "x", SWAP)
    far_low = lax.ppermute(x_low, "y", SWAP)
    stack = lambda top, low: jnp.concatenate([top, low], 0)
    blocks = stack(x_top, x_low), stack(y_top, y_low), stack(far_top, far_low)
    return blocks, later


def exchange(to_x, to_y, across):
    return (
        lax.ppermute(to_x, "x", SWAP),
        lax.ppermute(to_y, "y", SWAP),
        lax.ppermute(across, ("y", "x"), [(place, 3 - place) for place in range(4)]),
    )


def fold_cores(part):
    half = part.shape[0] // 2
    got = lax.ppermute(part[half:].astype(BF16), "c", SWAP)
    return (part[:half] + got.astype(F32)).astype(BF16)


def sum_planes(*parts):
    planes = lax.axis_size("z")
    rows = jnp.stack([part.reshape(planes, -1, part.shape[1]) for part in parts], 1)
    got = lax.all_to_all(rows, "z", 0, 0, tiled=True)
    return jnp.sum(got.astype(F32), 0)


def with_other_core(half):
    return jnp.concatenate([half, lax.ppermute(half, "c", SWAP)], 0)


def gather_rows(quarter):
    return with_other_core(lax.all_gather(quarter, "z", axis=0, tiled=True))


def on_device(tokens, cotangent, probe_seed, w_in, bias, w_out, left_in, left_out):
    coef = 0.9
    planes = lax.axis_size("z")
    at_z, at_y, at_x, core = (lax.axis_index(name) for name in EVERY)
    count, width = tokens.shape
    rows_in, hid_rep = w_in.shape
    rows_out = w_out.shape[0]
    piece = hid_rep // planes
    quarter = count // 4
    at_dp = at_z * 2 + at_y
    at_rep = at_x * 2 + core

    def own_quarter(array):
        return lax.dynamic_slice_in_dim(array, at_rep * quarter, quarter, 0)

    def rows_of(array, y_index):
        starts = [(2 * plane + y_index) * rows_in for plane in range(planes)]
        return jnp.concatenate(
            [lax.dynamic_slice_in_dim(array, start, rows_in, 1) for start in starts], 1
        )

    def units_of(array, y_index, x_other):
        start = (2 * x_other + y_index) * rows_out
        return lax.dynamic_slice_in_dim(array, start, rows_out, 1)

    left_one = left_in.astype(F32)
    slice_one = lax.dynamic_slice_in_dim(left_in, at_dp * rows_in, rows_in, 0)
    slice_two = lax.dynamic_slice_in_dim(left_out, at_dp * rows_out, rows_out, 0)
    p_part = times(slice_one, w_in)
    q_part = times(slice_two, w_out)
    slice_one = slice_one.astype(F32)
    slice_two = slice_two.astype(F32)
    sums = sum_over(
        jnp.concatenate([p_part, q_part, jnp.sum(slice_two * slice_two)[None]]), ("z",)
    )

    seeds = jnp.where(
        jnp.arange(planes)[:, None] == at_z, own_quarter(probe_seed)[None, :], 0
    ).reshape(-1)
    seeds = sum_over(seeds, ("z",))
    w_late, sums, seeds = tied((w_in, sums, seeds))
    in_z = lax.all_to_all(w_late, "z", 1, 0, tiled=True)
    bias_own = lax.dynamic_slice_in_dim(bias, at_z * piece, piece, 0)
    (out_x, out_y, out_d), (sums, seeds, bias_own) = spread(w_out, sums, seeds, bias_own)
    full_out = jnp.concatenate([in_order(w_out, out_y, at_y), in_order(out_x, out_d, at_y)], 0)

    def join_rows(own, other):
        first = jnp.where(at_y == 0, own, other).reshape(planes, 1, rows_in, piece)
        second = jnp.where(at_y == 0, other, own).reshape(planes, 1, rows_in, piece)
        return jnp.concatenate([first, second], 1).reshape(width, piece)

    tok_own = own_quarter(tokens)
    in_z, pair = tied((in_z, jnp.stack([tok_own, own_quarter(cotangent)])))
    (in_x, in_y, in_d), _ = spread(in_z)
    full_in = jnp.concatenate([join_rows(in_z, in_y), join_rows(in_x, in_d)], 1)

    sums = sum_over(sums, ("y",))
    p_vec = sums[:hid_rep]
    sums = sum_over(jnp.concatenate([sums[hid_rep:], jnp.sum(p_vec * p_vec)[None]]), ("c", "x"))
    q_vec = sums[:width]
    p_norm = sums[-1]
    q_norm = jnp.sum(q_vec * q_vec)
    scale_in = coef * jnp.sqrt(jnp.sum(left_one * left_one) / p_norm)
    scale_out = coef * jnp.sqrt(sums[-2] / q_norm)

    pair = lax.all_gather(pair, "z", axis=1)
    tok = with_other_core(pair[0].reshape(-1, width))
    cot = with_other_core(pair[1].reshape(-1, width))
    n = tok.shape[0]
    seeds = with_other_core(seeds)
    probe = probe_signs(seeds, width)
    bias_all = jnp.concatenate([bias_own, lax.ppermute(bias_own, "x", SWAP)])

    raw = times(jnp.concatenate([tok, probe], 0), full_in)
    raw_z = raw[:n]
    e_one = scale_in * raw[n:]
    tanh_z = jnp.tanh(scale_in * raw_z + bias_all)
    deriv = 1.0 - tanh_z * tanh_z
    act = tanh_z.astype(BF16)
    r_one = (e_one * deriv).astype(BF16)
    factors = n <= 4 * rows_out

    def exchange_units(array):
        parts = exchange(
            units_of(array, at_y, 1), units_of(array, 1 - at_y, 0), units_of(array, 1 - at_y, 1)
        )
        return (units_of(array, at_y, 0), *parts)

    j_pair = fold_cores(scale_out * times(r_one, full_out))
    j_pair, cot_late, seeds_late, probe_late, act_late = tied((j_pair, cot, seeds, probe, act))
    if factors:
        cot_rows = lax.all_gather(cot_late, ("x", "y"), axis=0, tiled=True)
        seeds_all = jnp.where(
            jnp.arange(4)[:, None] == at_x * 2 + at_y, seeds_late[None, :], 0
        ).reshape(-1)
        seeds_all = sum_over(seeds_all, ("x", "y")).reshape(4, n)
        act_units = exchange_units(act_late)
    backs = contract_cols(jnp.concatenate([probe_late, cot_late], 0), full_out)
    raw_b = backs[:n]
    raw_c = backs[n:]
    hd = deriv * (scale_out * raw_b)
    h_round = hd.astype(BF16)
    quarter_one = sum_planes(j_pair)[0].astype(BF16)
    quarter_one, h_round, raw_c = tied((quarter_one, h_round, raw_c))
    j_one = gather_rows(quarter_one)

    e_two = scale_in * times(j_one, full_in)
    r_two = (e_two * deriv).astype(BF16)
    j_pair = fold_cores(scale_out * times(r_two, full_out))
    j_pair, act_late = tied((j_pair, act_late))
    branch = fold_cores(scale_out * times(act_late, full_out))
    quarter_two = sum_planes(j_pair)[0].astype(BF16)
    if factors:
        quarter_two, branch, seeds_all, cot_rows, act_units = tied(
            (quarter_two, branch, seeds_all, cot_rows, act_units)
        )
    else:
        quarter_two, branch = tied((quarter_two, branch))
    j_two, branch = tied((gather_rows(quarter_two), branch))

    w_vec = (probe.astype(F32) - j_one.astype(F32) + j_two.astype(F32)).astype(BF16)
    e_three = scale_in * times(j_two, full_in)
    a_vec = e_one - e_two + e_three
    second = -2.0 * tanh_z * deriv
    dz_vec = scale_out * raw_c * deriv - a_vec * (scale_out * raw_b) * second
    dz_round = dz_vec.astype(BF16)
    g_round = (a_vec * deriv).astype(BF16)

    left_grad = jnp.concatenate([tok, w_vec], 0)
    right_grad = jnp.concatenate([dz_round, -h_round], 0)
    own_cols, other_cols = right_grad[:, :piece], right_grad[:, piece:]
    near, over = rows_of(left_grad, at_y), rows_of(left_grad, 1 - at_y)
    half = near.shape[1] // 2
    near_top, near_low = near[:, :half], near[:, half:]
    over_top, over_low = over[:, :half], over[:, half:]
    across_x = contract_rows(over_top, other_cols).astype(BF16)
    across_y = contract_rows(over_low, other_cols).astype(BF16)
    across_x, across_y, own_cols, other_cols = tied((across_x, across_y, own_cols, other_cols))
    across_x = lax.ppermute(across_x, "x", SWAP)
    across_y = lax.ppermute(across_y, "y", SWAP)
    x_top = lax.ppermute(contract_rows(near_top, other_cols).astype(BF16), "x", SWAP)
    y_low = lax.ppermute(contract_rows(over_low, own_cols).astype(BF16), "y", SWAP)
    dx = fold_cores(scale_in * contract_cols(dz_round, full_in))
    ends = sum_planes(branch, dx)
    ends = jnp.stack([tok_own.astype(F32) + ends[0], ends[1]]).astype(BF16)
    across_x, across_y, g_late, a_late, e_late, dz_late = tied(
        (across_x, across_y, g_round, a_vec, e_three, dz_round)
    )
    terms = jnp.sum((e_one - e_two / 2.0 + e_late / 3.0) * hd, axis=1)
    inner_one = jnp.sum(dz_late.astype(F32) * raw_z - h_round.astype(F32) * (a_late / scale_in))
    inner_two = jnp.sum(act.astype(F32) * raw_c - g_late.astype(F32) * raw_b)
    inner = jnp.stack([inner_one, inner_two])
    tail = jnp.concatenate([terms, inner])
    got = lax.ppermute(tail, "c", SWAP)
    got = jnp.concatenate([got[n // 2 : n], got[: n // 2], got[n:]])
    tail = sum_over(tail + got, ("z",))
    ends = lax.all_gather(ends, ("x", "c"), axis=1, tiled=True)

    x_low = contract_rows(near_low, other_cols) + across_y.astype(F32)
    y_top = contract_rows(over_top, own_cols) + across_x.astype(F32)
    x_low = lax.ppermute(x_low.astype(BF16), "x", SWAP)
    y_top = lax.ppermute(y_top.astype(BF16), "y", SWAP)
    top = contract_rows(near_top, own_cols) + x_top.astype(F32) + y_top.astype(F32)
    low = contract_rows(near_low, own_cols) + x_low.astype(F32) + y_low.astype(F32)
    block = jnp.concatenate([top.astype(BF16), low.astype(BF16)], 0)
    block, tail, g_late = tied((block, tail, g_late))
    grad_one = lax.all_to_all(block, "z", 0, 1, tiled=True).astype(F32)

    if factors:
        own_act, x_act, y_act, d_act = act_units
        act_rows = in_order(
            in_order(own_act, y_act, at_y), in_order(x_act, d_act, at_y), at_x
        )
        grad_two = contract_rows(act_rows, cot_rows)
        at_group = at_x * 2 + at_y
        seeds_near = [
            lax.dynamic_index_in_dim(seeds_all, at_group ^ other, 0, keepdims=False)
            for other in (0, 2, 1, 3)
        ]
        probe_rows = probe_signs(jnp.concatenate(seeds_near), width)
        g_rows = jnp.concatenate(exchange_units(g_late), 0)
        grad_two = grad_two - contract_rows(g_rows, probe_rows)
    else:

        def block_two(y_index, x_other):
            grad = contract_rows(units_of(act, y_index, x_other), cot)
            return grad - contract_rows(units_of(g_late, y_index, x_other), probe)

        parts = exchange(
            block_two(at_y, 1).astype(BF16),
            block_two(1 - at_y, 0).astype(BF16),
            block_two(1 - at_y, 1).astype(BF16),
        )
        grad_two = block_two(at_y, 0) + sum(part.astype(F32) for part in parts)

    output = ends[0]
    grad_tokens = cotangent.astype(F32) + ends[1].astype(F32)

    terms = lax.dynamic_index_in_dim(tail[:n].reshape(2, planes, quarter), at_z, 1, keepdims=False)
    terms = in_order(terms[0], terms[1], core)
    tail = jnp.concatenate([tail[n:], terms])
    tail_x = lax.ppermute(tail, "x", SWAP)
    logdet = in_order(tail[2:], tail_x[2:], at_x)
    inner = sum_over(tail[:2] + tail_x[:2], ("y",))

    grad_in = scale_in * (grad_one - inner[0] * slice_one[:, None] * p_vec[None, :] / p_norm)
    grad_out = scale_out * (grad_two - inner[1] * slice_two[:, None] * q_vec[None, :] / q_norm)
    return (output, logdet, grad_tokens, grad_in, grad_out)


def solution(mesh):
    fine = Mesh(
        mesh.devices.reshape(mesh.shape["dp"] // 2, 2, mesh.shape["rep"] // 2, 2), EVERY
    )
    dp, rep = ("z", "y"), ("x", "c")
    placed = (
        P(dp, None),
        P(dp, None),
        P(dp),
        P(dp, rep),
        P(rep),
        P(rep + dp, None),
        P(),
        P(rep),
    )
    return jax.shard_map(
        on_device,
        mesh=fine,
        in_specs=placed,
        out_specs=(P(dp, None), P(dp), P(dp, None), P(dp, rep), P(rep + dp, None)),
        check_vma=False,
    )
```

```python
import jax
import jax.numpy as jnp
from jax import lax
from jax.sharding import Mesh
from jax.sharding import PartitionSpec as P

F32 = jnp.float32
BF16 = jnp.bfloat16
EVERY = ("z", "y", "x", "c")
SWAP = [(0, 1), (1, 0)]


def probe_signs(seeds, width):
    columns = jnp.arange(width, dtype=jnp.int32)
    mixed = seeds[:, None] * 747796405 + columns[None, :] * 1640531527
    mixed = mixed ^ lax.shift_right_logical(mixed, jnp.full_like(mixed, 16))
    mixed = mixed * 668265261
    mixed = mixed ^ lax.shift_right_logical(mixed, jnp.full_like(mixed, 15))
    lowbit = jnp.bitwise_and(lax.shift_right_logical(mixed, jnp.full_like(mixed, 7)), 1)
    return (1 - 2 * lowbit).astype(F32).astype(BF16)


def times(left, right):
    return jnp.dot(left, right, preferred_element_type=F32)


def contract_rows(left, right):
    return lax.dot_general(left, right, (((0,), (0,)), ((), ())), preferred_element_type=F32)


def contract_cols(left, right):
    return lax.dot_general(left, right, (((1,), (1,)), ((), ())), preferred_element_type=F32)


def in_order(own, other, index):
    first = jnp.where(index == 0, own, other)
    second = jnp.where(index == 0, other, own)
    return jnp.concatenate([first, second], 0)


def sum_over(values, names):
    for name in names:
        size, step = lax.axis_size(name), 1
        while step < size:
            pairs = [(place, place ^ step) for place in range(size)]
            values = values + lax.ppermute(values, name, pairs)
            step *= 2
    return values


tied = lax.optimization_barrier


def spread(block, *later):
    half = block.shape[0] // 2
    x_low = lax.ppermute(block[half:], "x", SWAP)
    y_top = lax.ppermute(block[:half], "y", SWAP)
    x_top = lax.ppermute(block[:half], "x", SWAP)
    y_low = lax.ppermute(block[half:], "y", SWAP)
    x_low, y_top, later = tied((x_low, y_top, later))
    far_top = lax.ppermute(y_top, "x", SWAP)
    far_low = lax.ppermute(x_low, "y", SWAP)
    stack = lambda top, low: jnp.concatenate([top, low], 0)
    blocks = stack(x_top, x_low), stack(y_top, y_low), stack(far_top, far_low)
    return blocks, later


def exchange(to_x, to_y, across):
    return (
        lax.ppermute(to_x, "x", SWAP),
        lax.ppermute(to_y, "y", SWAP),
        lax.ppermute(across, ("y", "x"), [(place, 3 - place) for place in range(4)]),
    )


def fold_cores(part):
    half = part.shape[0] // 2
    got = lax.ppermute(part[half:].astype(BF16), "c", SWAP)
    return (part[:half] + got.astype(F32)).astype(BF16)


def sum_planes(rows):
    planes = lax.axis_size("z")
    got = lax.all_to_all(rows, "z", 0, 0, tiled=True)
    return jnp.sum(got.reshape(planes, rows.shape[0] // planes, -1).astype(F32), 0)


def with_other_core(half):
    return jnp.concatenate([half, lax.ppermute(half, "c", SWAP)], 0)


def gather_rows(quarter):
    return with_other_core(lax.all_gather(quarter, "z", axis=0, tiled=True))


def on_device(tokens, cotangent, probe_seed, w_in, bias, w_out, left_in, left_out):
    coef = 0.9
    planes = lax.axis_size("z")
    at_z, at_y, at_x, core = (lax.axis_index(name) for name in EVERY)
    count, width = tokens.shape
    rows_in, hid_rep = w_in.shape
    rows_out = w_out.shape[0]
    piece = hid_rep // planes
    quarter = count // 4
    at_dp = at_z * 2 + at_y
    at_rep = at_x * 2 + core

    def own_quarter(array):
        return lax.dynamic_slice_in_dim(array, at_rep * quarter, quarter, 0)

    def rows_of(array, y_index):
        starts = [(2 * plane + y_index) * rows_in for plane in range(planes)]
        return jnp.concatenate(
            [lax.dynamic_slice_in_dim(array, start, rows_in, 1) for start in starts], 1
        )

    def units_of(array, y_index, x_other):
        start = (2 * x_other + y_index) * rows_out
        return lax.dynamic_slice_in_dim(array, start, rows_out, 1)

    left_one = left_in.astype(F32)
    slice_one = lax.dynamic_slice_in_dim(left_in, at_dp * rows_in, rows_in, 0)
    slice_two = lax.dynamic_slice_in_dim(left_out, at_dp * rows_out, rows_out, 0)
    p_part = times(slice_one, w_in)
    q_part = times(slice_two, w_out)
    slice_one = slice_one.astype(F32)
    slice_two = slice_two.astype(F32)
    sums = sum_over(
        jnp.concatenate([p_part, q_part, jnp.sum(slice_two * slice_two)[None]]), ("z",)
    )

    seeds = jnp.where(
        jnp.arange(planes)[:, None] == at_z, own_quarter(probe_seed)[None, :], 0
    ).reshape(-1)
    seeds = sum_over(seeds, ("z",))
    w_late, sums, seeds = tied((w_in, sums, seeds))
    in_z = lax.all_to_all(w_late, "z", 1, 0, tiled=True)
    bias_own = lax.dynamic_slice_in_dim(bias, at_z * piece, piece, 0)
    (out_x, out_y, out_d), (sums, seeds, bias_own) = spread(w_out, sums, seeds, bias_own)
    full_out = jnp.concatenate([in_order(w_out, out_y, at_y), in_order(out_x, out_d, at_y)], 0)

    def join_rows(own, other):
        first = jnp.where(at_y == 0, own, other).reshape(planes, 1, rows_in, piece)
        second = jnp.where(at_y == 0, other, own).reshape(planes, 1, rows_in, piece)
        return jnp.concatenate([first, second], 1).reshape(width, piece)

    tok_own = own_quarter(tokens)
    in_z, pair = tied((in_z, jnp.stack([tok_own, own_quarter(cotangent)])))
    sums = sum_over(sums, ("y",))
    seeds = with_other_core(seeds)
    (in_x, in_y, in_d), (sums, bias_own) = spread(in_z, sums, bias_own)

    p_vec = sums[:hid_rep]
    sums = sum_over(jnp.concatenate([sums[hid_rep:], jnp.sum(p_vec * p_vec)[None]]), ("c", "x"))
    q_vec = sums[:width]
    p_norm = sums[-1]
    q_norm = jnp.sum(q_vec * q_vec)
    scale_in = coef * jnp.sqrt(jnp.sum(left_one * left_one) / p_norm)
    scale_out = coef * jnp.sqrt(sums[-2] / q_norm)

    pair = lax.all_gather(pair, "z", axis=1)
    tok = with_other_core(pair[0].reshape(-1, width))
    cot = with_other_core(pair[1].reshape(-1, width))
    n = tok.shape[0]
    probe = probe_signs(seeds, width)
    bias_all = jnp.concatenate([bias_own, lax.ppermute(bias_own, "x", SWAP)])
    in_d, tok, cot, probe = tied((in_d, tok, cot, probe))
    full_in = jnp.concatenate([join_rows(in_z, in_y), join_rows(in_x, in_d)], 1)

    raw = times(jnp.concatenate([tok, probe], 0), full_in)
    raw_z = raw[:n]
    e_one = scale_in * raw[n:]
    tanh_z = jnp.tanh(scale_in * raw_z + bias_all)
    deriv = 1.0 - tanh_z * tanh_z
    act = tanh_z.astype(BF16)
    r_one = (e_one * deriv).astype(BF16)
    factors = n <= 4 * rows_out

    def exchange_units(array):
        parts = exchange(
            units_of(array, at_y, 1), units_of(array, 1 - at_y, 0), units_of(array, 1 - at_y, 1)
        )
        return (units_of(array, at_y, 0), *parts)

    j_pair = fold_cores(scale_out * times(r_one, full_out))
    j_pair, cot_late, seeds_late, probe_late, act_late = tied((j_pair, cot, seeds, probe, act))
    if factors:
        cot_rows = lax.all_gather(cot_late, ("x", "y"), axis=0, tiled=True)
        seeds_all = jnp.where(
            jnp.arange(4)[:, None] == at_x * 2 + at_y, seeds_late[None, :], 0
        ).reshape(-1)
        seeds_all = sum_over(seeds_all, ("x", "y")).reshape(4, n)
        act_units = exchange_units(act_late)
    backs = contract_cols(jnp.concatenate([probe_late, cot_late], 0), full_out)
    raw_b = backs[:n]
    raw_c = backs[n:]
    hd = deriv * (scale_out * raw_b)
    h_round = hd.astype(BF16)
    quarter_one = sum_planes(j_pair).astype(BF16)
    quarter_one, h_round, raw_c = tied((quarter_one, h_round, raw_c))
    j_one = gather_rows(quarter_one)

    e_two = scale_in * times(j_one, full_in)
    r_two = (e_two * deriv).astype(BF16)
    j_pair = fold_cores(scale_out * times(r_two, full_out))
    j_pair, act_late = tied((j_pair, act_late))
    branch = fold_cores(scale_out * times(act_late, full_out))
    quarter_two = sum_planes(j_pair).astype(BF16)
    if factors:
        quarter_two, branch, seeds_all, cot_rows, act_units = tied(
            (quarter_two, branch, seeds_all, cot_rows, act_units)
        )
    else:
        quarter_two, branch = tied((quarter_two, branch))
    j_two, branch = tied((gather_rows(quarter_two), branch))

    w_vec = (probe.astype(F32) - j_one.astype(F32) + j_two.astype(F32)).astype(BF16)
    e_three = scale_in * times(j_two, full_in)
    a_vec = e_one - e_two + e_three
    second = -2.0 * tanh_z * deriv
    dz_vec = scale_out * raw_c * deriv - a_vec * (scale_out * raw_b) * second
    dz_round = dz_vec.astype(BF16)
    g_round = (a_vec * deriv).astype(BF16)

    left_grad = jnp.concatenate([tok, w_vec], 0)
    right_grad = jnp.concatenate([dz_round, -h_round], 0)
    own_cols, other_cols = right_grad[:, :piece], right_grad[:, piece:]
    near, over = rows_of(left_grad, at_y), rows_of(left_grad, 1 - at_y)
    half = near.shape[1] // 2
    near_top, near_low = near[:, :half], near[:, half:]
    over_top, over_low = over[:, :half], over[:, half:]
    across_x = contract_rows(over_top, other_cols).astype(BF16)
    across_y = contract_rows(over_low, other_cols).astype(BF16)
    across_x, across_y, g_late, a_late, e_late, dz_late = tied(
        (across_x, across_y, g_round, a_vec, e_three, dz_round)
    )
    across_x = lax.ppermute(across_x, "x", SWAP)
    across_y = lax.ppermute(across_y, "y", SWAP)
    dx = fold_cores(scale_in * contract_cols(dz_late, full_in))
    terms = jnp.sum((e_one - e_two / 2.0 + e_late / 3.0) * hd, axis=1)
    inner_one = jnp.sum(dz_late.astype(F32) * raw_z - h_round.astype(F32) * (a_late / scale_in))
    inner_two = jnp.sum(act.astype(F32) * raw_c - g_late.astype(F32) * raw_b)
    inner = jnp.stack([inner_one, inner_two])
    tail = jnp.concatenate([terms, inner])
    got = lax.ppermute(tail, "c", SWAP)
    tail = tail + jnp.concatenate([got[n // 2 : n], got[: n // 2], got[n:]])
    across_x, across_y, own_cols, other_cols, dx, tail = tied(
        (across_x, across_y, own_cols, other_cols, dx, tail)
    )
    x_top = lax.ppermute(contract_rows(near_top, other_cols).astype(BF16), "x", SWAP)
    y_low = lax.ppermute(contract_rows(over_low, own_cols).astype(BF16), "y", SWAP)
    x_low = contract_rows(near_low, other_cols) + across_y.astype(F32)
    y_top = contract_rows(over_top, own_cols) + across_x.astype(F32)
    x_low = lax.ppermute(x_low.astype(BF16), "x", SWAP)
    y_top = lax.ppermute(y_top.astype(BF16), "y", SWAP)
    ends = jnp.stack([rows.reshape(planes, quarter, width) for rows in (branch, dx)], 1)
    ends = lax.psum_scatter(ends, "z", scatter_dimension=0, tiled=True)[0].astype(F32)
    ends = jnp.stack([tok_own.astype(F32) + ends[0], ends[1]]).astype(BF16)
    ends = lax.all_gather(ends, ("x", "c"), axis=1, tiled=True)
    tail = sum_over(tail, ("z",))
    top = contract_rows(near_top, own_cols) + x_top.astype(F32) + y_top.astype(F32)
    low = contract_rows(near_low, own_cols) + x_low.astype(F32) + y_low.astype(F32)
    block = jnp.concatenate([top.astype(BF16), low.astype(BF16)], 0)
    if factors:
        block, tail, g_late, act_units = tied((block, tail, g_late, act_units))
    else:
        block, tail, g_late = tied((block, tail, g_late))
    grad_one = lax.all_to_all(block, "z", 0, 1, tiled=True).astype(F32)

    if factors:
        own_act, x_act, y_act, d_act = act_units
        act_rows = in_order(
            in_order(own_act, y_act, at_y), in_order(x_act, d_act, at_y), at_x
        )
        grad_two = contract_rows(act_rows, cot_rows)
        at_group = at_x * 2 + at_y
        seeds_near = [
            lax.dynamic_index_in_dim(seeds_all, at_group ^ other, 0, keepdims=False)
            for other in (0, 2, 1, 3)
        ]
        probe_rows = probe_signs(jnp.concatenate(seeds_near), width)
        g_rows = jnp.concatenate(exchange_units(g_late), 0)
        grad_two = grad_two - contract_rows(g_rows, probe_rows)
    else:

        def block_two(y_index, x_other):
            grad = contract_rows(units_of(act, y_index, x_other), cot)
            return grad - contract_rows(units_of(g_late, y_index, x_other), probe)

        parts = exchange(
            block_two(at_y, 1).astype(BF16),
            block_two(1 - at_y, 0).astype(BF16),
            block_two(1 - at_y, 1).astype(BF16),
        )
        grad_two = block_two(at_y, 0) + sum(part.astype(F32) for part in parts)

    output = ends[0]
    grad_tokens = cotangent.astype(F32) + ends[1].astype(F32)

    terms = lax.dynamic_index_in_dim(tail[:n].reshape(2, planes, quarter), at_z, 1, keepdims=False)
    terms = in_order(terms[0], terms[1], core)
    tail = jnp.concatenate([tail[n:], terms])
    tail_x = lax.ppermute(tail, "x", SWAP)
    logdet = in_order(tail[2:], tail_x[2:], at_x)
    inner = sum_over(tail[:2] + tail_x[:2], ("y",))

    grad_in = scale_in * (grad_one - inner[0] * slice_one[:, None] * p_vec[None, :] / p_norm)
    grad_out = scale_out * (grad_two - inner[1] * slice_two[:, None] * q_vec[None, :] / q_norm)
    return (output, logdet, grad_tokens, grad_in, grad_out)


def solution(mesh):
    fine = Mesh(
        mesh.devices.reshape(mesh.shape["dp"] // 2, 2, mesh.shape["rep"] // 2, 2), EVERY
    )
    dp, rep = ("z", "y"), ("x", "c")
    placed = (
        P(dp, None),
        P(dp, None),
        P(dp),
        P(dp, rep),
        P(rep),
        P(rep + dp, None),
        P(),
        P(rep),
    )
    return jax.shard_map(
        on_device,
        mesh=fine,
        in_specs=placed,
        out_specs=(P(dp, None), P(dp), P(dp, None), P(dp, rep), P(rep + dp, None)),
        check_vma=False,
    )
```

```python
import jax
import jax.numpy as jnp
from jax import lax
from jax.sharding import Mesh
from jax.sharding import PartitionSpec as P

F32 = jnp.float32
BF16 = jnp.bfloat16
EVERY = ("z", "y", "x", "c")
SWAP = [(0, 1), (1, 0)]


def probe_signs(seeds, width):
    columns = jnp.arange(width, dtype=jnp.int32)
    mixed = seeds[:, None] * 747796405 + columns[None, :] * 1640531527
    mixed = mixed ^ lax.shift_right_logical(mixed, jnp.full_like(mixed, 16))
    mixed = mixed * 668265261
    mixed = mixed ^ lax.shift_right_logical(mixed, jnp.full_like(mixed, 15))
    lowbit = jnp.bitwise_and(lax.shift_right_logical(mixed, jnp.full_like(mixed, 7)), 1)
    return (1 - 2 * lowbit).astype(F32).astype(BF16)


def times(left, right):
    return jnp.dot(left, right, preferred_element_type=F32)


def contract_rows(left, right):
    return lax.dot_general(left, right, (((0,), (0,)), ((), ())), preferred_element_type=F32)


def contract_cols(left, right):
    return lax.dot_general(left, right, (((1,), (1,)), ((), ())), preferred_element_type=F32)


def in_order(own, other, index):
    first = jnp.where(index == 0, own, other)
    second = jnp.where(index == 0, other, own)
    return jnp.concatenate([first, second], 0)


def sum_over(values, names):
    for name in names:
        size, step = lax.axis_size(name), 1
        while step < size:
            pairs = [(place, place ^ step) for place in range(size)]
            values = values + lax.ppermute(values, name, pairs)
            step *= 2
    return values


tied = lax.optimization_barrier


def spread(block, *later):
    half = block.shape[0] // 2
    x_low = lax.ppermute(block[half:], "x", SWAP)
    y_top = lax.ppermute(block[:half], "y", SWAP)
    x_top = lax.ppermute(block[:half], "x", SWAP)
    y_low = lax.ppermute(block[half:], "y", SWAP)
    x_low, y_top, later = tied((x_low, y_top, later))
    far_top = lax.ppermute(y_top, "x", SWAP)
    far_low = lax.ppermute(x_low, "y", SWAP)
    stack = lambda top, low: jnp.concatenate([top, low], 0)
    blocks = stack(x_top, x_low), stack(y_top, y_low), stack(far_top, far_low)
    return blocks, later


def exchange(to_x, to_y, across):
    return (
        lax.ppermute(to_x, "x", SWAP),
        lax.ppermute(to_y, "y", SWAP),
        lax.ppermute(across, ("y", "x"), [(place, 3 - place) for place in range(4)]),
    )


def fold_cores(part):
    half = part.shape[0] // 2
    got = lax.ppermute(part[half:].astype(BF16), "c", SWAP)
    return (part[:half] + got.astype(F32)).astype(BF16)


def sum_planes(rows):
    planes = lax.axis_size("z")
    got = lax.all_to_all(rows, "z", 0, 0, tiled=True)
    return jnp.sum(got.reshape(planes, rows.shape[0] // planes, -1).astype(F32), 0)


def with_other_core(half):
    return jnp.concatenate([half, lax.ppermute(half, "c", SWAP)], 0)


def gather_rows(quarter):
    return with_other_core(lax.all_gather(quarter, "z", axis=0, tiled=True))


def on_device(tokens, cotangent, probe_seed, w_in, bias, w_out, left_in, left_out):
    coef = 0.9
    planes = lax.axis_size("z")
    at_z, at_y, at_x, core = (lax.axis_index(name) for name in EVERY)
    count, width = tokens.shape
    rows_in, hid_rep = w_in.shape
    rows_out = w_out.shape[0]
    piece = hid_rep // planes
    quarter = count // 4
    at_dp = at_z * 2 + at_y
    at_rep = at_x * 2 + core

    def own_quarter(array):
        return lax.dynamic_slice_in_dim(array, at_rep * quarter, quarter, 0)

    def rows_of(array, y_index):
        starts = [(2 * plane + y_index) * rows_in for plane in range(planes)]
        return jnp.concatenate(
            [lax.dynamic_slice_in_dim(array, start, rows_in, 1) for start in starts], 1
        )

    def units_of(array, y_index, x_other):
        start = (2 * x_other + y_index) * rows_out
        return lax.dynamic_slice_in_dim(array, start, rows_out, 1)

    left_one = left_in.astype(F32)
    slice_one = lax.dynamic_slice_in_dim(left_in, at_dp * rows_in, rows_in, 0)
    slice_two = lax.dynamic_slice_in_dim(left_out, at_dp * rows_out, rows_out, 0)
    p_part = times(slice_one, w_in)
    q_part = times(slice_two, w_out)
    slice_one = slice_one.astype(F32)
    slice_two = slice_two.astype(F32)
    sums = sum_over(
        jnp.concatenate([p_part, q_part, jnp.sum(slice_two * slice_two)[None]]), ("z",)
    )

    seeds = jnp.where(
        jnp.arange(planes)[:, None] == at_z, own_quarter(probe_seed)[None, :], 0
    ).reshape(-1)
    seeds = sum_over(seeds, ("z",))
    w_late, sums, seeds = tied((w_in, sums, seeds))
    in_z = lax.all_to_all(w_late, "z", 1, 0, tiled=True)
    bias_own = lax.dynamic_slice_in_dim(bias, at_z * piece, piece, 0)
    (out_x, out_y, out_d), (sums, seeds, bias_own) = spread(w_out, sums, seeds, bias_own)
    full_out = jnp.concatenate([in_order(w_out, out_y, at_y), in_order(out_x, out_d, at_y)], 0)

    def join_rows(own, other):
        first = jnp.where(at_y == 0, own, other).reshape(planes, 1, rows_in, piece)
        second = jnp.where(at_y == 0, other, own).reshape(planes, 1, rows_in, piece)
        return jnp.concatenate([first, second], 1).reshape(width, piece)

    tok_own = own_quarter(tokens)
    in_z, pair = tied((in_z, jnp.stack([tok_own, own_quarter(cotangent)])))
    sums = sum_over(sums, ("y",))
    seeds = with_other_core(seeds)
    (in_x, in_y, in_d), (sums, bias_own) = spread(in_z, sums, bias_own)

    p_vec = sums[:hid_rep]
    sums = sum_over(jnp.concatenate([sums[hid_rep:], jnp.sum(p_vec * p_vec)[None]]), ("c", "x"))
    q_vec = sums[:width]
    p_norm = sums[-1]
    q_norm = jnp.sum(q_vec * q_vec)
    scale_in = coef * jnp.sqrt(jnp.sum(left_one * left_one) / p_norm)
    scale_out = coef * jnp.sqrt(sums[-2] / q_norm)

    pair = lax.all_gather(pair, "z", axis=1)
    tok = with_other_core(pair[0].reshape(-1, width))
    cot = with_other_core(pair[1].reshape(-1, width))
    n = tok.shape[0]
    probe = probe_signs(seeds, width)
    bias_all = jnp.concatenate([bias_own, lax.ppermute(bias_own, "x", SWAP)])
    in_d, tok, cot, probe = tied((in_d, tok, cot, probe))
    full_in = jnp.concatenate([join_rows(in_z, in_y), join_rows(in_x, in_d)], 1)

    raw = times(jnp.concatenate([tok, probe], 0), full_in)
    raw_z = raw[:n]
    e_one = scale_in * raw[n:]
    tanh_z = jnp.tanh(scale_in * raw_z + bias_all)
    deriv = 1.0 - tanh_z * tanh_z
    act = tanh_z.astype(BF16)
    r_one = (e_one * deriv).astype(BF16)
    factors = n <= 4 * rows_out

    def exchange_units(array):
        parts = exchange(
            units_of(array, at_y, 1), units_of(array, 1 - at_y, 0), units_of(array, 1 - at_y, 1)
        )
        return (units_of(array, at_y, 0), *parts)

    j_pair = fold_cores(scale_out * times(r_one, full_out))
    j_pair, cot_late, seeds_late, probe_late, act_late = tied((j_pair, cot, seeds, probe, act))
    if factors:
        cot_rows = lax.all_gather(cot_late, ("x", "y"), axis=0, tiled=True)
        seeds_all = jnp.where(
            jnp.arange(4)[:, None] == at_x * 2 + at_y, seeds_late[None, :], 0
        ).reshape(-1)
        seeds_all = sum_over(seeds_all, ("x", "y")).reshape(4, n)
        act_units = exchange_units(act_late)
    backs = contract_cols(jnp.concatenate([probe_late, cot_late], 0), full_out)
    raw_b = backs[:n]
    raw_c = backs[n:]
    hd = deriv * (scale_out * raw_b)
    h_round = hd.astype(BF16)
    quarter_one = sum_planes(j_pair).astype(BF16)
    quarter_one, h_round, raw_c = tied((quarter_one, h_round, raw_c))
    j_one = gather_rows(quarter_one)

    e_two = scale_in * times(j_one, full_in)
    r_two = (e_two * deriv).astype(BF16)
    j_pair = fold_cores(scale_out * times(r_two, full_out))
    j_pair, act_late = tied((j_pair, act_late))
    branch = fold_cores(scale_out * times(act_late, full_out))
    quarter_two = sum_planes(j_pair).astype(BF16)
    if factors:
        quarter_two, branch, seeds_all, cot_rows, act_units = tied(
            (quarter_two, branch, seeds_all, cot_rows, act_units)
        )
    else:
        quarter_two, branch = tied((quarter_two, branch))
    j_two, branch = tied((gather_rows(quarter_two), branch))

    w_vec = (probe.astype(F32) - j_one.astype(F32) + j_two.astype(F32)).astype(BF16)
    e_three = scale_in * times(j_two, full_in)
    a_vec = e_one - e_two + e_three
    second = -2.0 * tanh_z * deriv
    dz_vec = scale_out * raw_c * deriv - a_vec * (scale_out * raw_b) * second
    dz_round = dz_vec.astype(BF16)
    g_round = (a_vec * deriv).astype(BF16)

    left_grad = jnp.concatenate([tok, w_vec], 0)
    right_grad = jnp.concatenate([dz_round, -h_round], 0)
    own_cols, other_cols = right_grad[:, :piece], right_grad[:, piece:]
    near, over = rows_of(left_grad, at_y), rows_of(left_grad, 1 - at_y)
    half = near.shape[1] // 2
    near_top, near_low = near[:, :half], near[:, half:]
    over_top, over_low = over[:, :half], over[:, half:]
    across_x = contract_rows(over_top, other_cols).astype(BF16)
    across_y = contract_rows(over_low, other_cols).astype(BF16)
    across_x, across_y, g_late, a_late, e_late, dz_late = tied(
        (across_x, across_y, g_round, a_vec, e_three, dz_round)
    )
    across_x = lax.ppermute(across_x, "x", SWAP)
    across_y = lax.ppermute(across_y, "y", SWAP)
    dx = fold_cores(scale_in * contract_cols(dz_late, full_in))
    terms = jnp.sum((e_one - e_two / 2.0 + e_late / 3.0) * hd, axis=1)
    inner_one = jnp.sum(dz_late.astype(F32) * raw_z - h_round.astype(F32) * (a_late / scale_in))
    inner_two = jnp.sum(act.astype(F32) * raw_c - g_late.astype(F32) * raw_b)
    inner = jnp.stack([inner_one, inner_two])
    tail = jnp.concatenate([terms, inner])
    got = lax.ppermute(tail, "c", SWAP)
    tail = tail + jnp.concatenate([got[n // 2 : n], got[: n // 2], got[n:]])
    across_x, across_y, own_cols, other_cols, dx, tail = tied(
        (across_x, across_y, own_cols, other_cols, dx, tail)
    )
    x_top = lax.ppermute(contract_rows(near_top, other_cols).astype(BF16), "x", SWAP)
    y_low = lax.ppermute(contract_rows(over_low, own_cols).astype(BF16), "y", SWAP)
    x_low = contract_rows(near_low, other_cols) + across_y.astype(F32)
    y_top = contract_rows(over_top, own_cols) + across_x.astype(F32)
    x_low = lax.ppermute(x_low.astype(BF16), "x", SWAP)
    y_top = lax.ppermute(y_top.astype(BF16), "y", SWAP)
    ends = jnp.stack([rows.reshape(planes, quarter, width) for rows in (branch, dx)], 1)
    ends = lax.psum_scatter(ends, "z", scatter_dimension=0, tiled=True)[0].astype(F32)
    ends = jnp.stack([tok_own.astype(F32) + ends[0], ends[1]]).astype(BF16)
    ends = lax.all_gather(ends, ("x", "c"), axis=1, tiled=True)
    tail = sum_over(tail, ("z",))
    top = contract_rows(near_top, own_cols) + x_top.astype(F32) + y_top.astype(F32)
    low = contract_rows(near_low, own_cols) + x_low.astype(F32) + y_low.astype(F32)
    block = jnp.concatenate([top.astype(BF16), low.astype(BF16)], 0)
    if factors:
        block, tail, g_late, act_units = tied((block, tail, g_late, act_units))
    else:
        block, tail, g_late = tied((block, tail, g_late))
    grad_one = lax.all_to_all(block, "z", 0, 1, tiled=True).astype(F32)
    terms = lax.dynamic_index_in_dim(tail[:n].reshape(2, planes, quarter), at_z, 1, keepdims=False)
    terms = in_order(terms[0], terms[1], core)
    tail = jnp.concatenate([tail[n:], terms])
    tail_x, g_late = tied((lax.ppermute(tail, "x", SWAP), g_late))

    if factors:
        own_act, x_act, y_act, d_act = act_units
        act_rows = in_order(
            in_order(own_act, y_act, at_y), in_order(x_act, d_act, at_y), at_x
        )
        grad_two = contract_rows(act_rows, cot_rows)
        at_group = at_x * 2 + at_y
        seeds_near = [
            lax.dynamic_index_in_dim(seeds_all, at_group ^ other, 0, keepdims=False)
            for other in (0, 2, 1, 3)
        ]
        probe_rows = probe_signs(jnp.concatenate(seeds_near), width)
        g_rows = jnp.concatenate(exchange_units(g_late), 0)
        grad_two = grad_two - contract_rows(g_rows, probe_rows)
    else:

        def block_two(y_index, x_other):
            grad = contract_rows(units_of(act, y_index, x_other), cot)
            return grad - contract_rows(units_of(g_late, y_index, x_other), probe)

        parts = exchange(
            block_two(at_y, 1).astype(BF16),
            block_two(1 - at_y, 0).astype(BF16),
            block_two(1 - at_y, 1).astype(BF16),
        )
        grad_two = block_two(at_y, 0) + sum(part.astype(F32) for part in parts)

    output = ends[0]
    grad_tokens = cotangent.astype(F32) + ends[1].astype(F32)

    logdet = in_order(tail[2:], tail_x[2:], at_x)
    inner = sum_over(tail[:2] + tail_x[:2], ("y",))

    grad_in = scale_in * (grad_one - inner[0] * slice_one[:, None] * p_vec[None, :] / p_norm)
    grad_out = scale_out * (grad_two - inner[1] * slice_two[:, None] * q_vec[None, :] / q_norm)
    return (output, logdet, grad_tokens, grad_in, grad_out)


def solution(mesh):
    fine = Mesh(
        mesh.devices.reshape(mesh.shape["dp"] // 2, 2, mesh.shape["rep"] // 2, 2), EVERY
    )
    dp, rep = ("z", "y"), ("x", "c")
    placed = (
        P(dp, None),
        P(dp, None),
        P(dp),
        P(dp, rep),
        P(rep),
        P(rep + dp, None),
        P(),
        P(rep),
    )
    return jax.shard_map(
        on_device,
        mesh=fine,
        in_specs=placed,
        out_specs=(P(dp, None), P(dp), P(dp, None), P(dp, rep), P(rep + dp, None)),
        check_vma=False,
    )
```
